512 devices in a mesh: seq: 64 (over x, y, z_hi, core), chan: 8 (over z_lo).
Axes of the slice: x: 4, y: 4, z: 16 (z_hi: 2, z_lo: 8; z = z_hi * 8 + z_lo), core: 2. Of those that a mesh axis runs over, the one named last changes fastest.
Arguments:
- tokens: bfloat16 [16384, 4096], P('seq', 'chan'), may hold values from -6 to 6
- w_in: bfloat16 [4096, 3, 4096], P('seq', None, 'chan'), may hold values from -0.09375 to 0.09375
- short_taps: float32 [3, 3, 4096], P(None, None, 'chan'), may hold values from -3 to 3
- residues: float32 [16, 4096], P(None, 'chan'), may hold values from -0.046875 to 0.046875
- poles: float32 [16, 4096], P(None, 'chan'), may hold values from 0.3 to 512
- skip_gain: float32 [4096], P('chan'), may hold values from 0.5 to 1.5
Outputs:
- mixed: bfloat16 [16384, 4096], P('seq', 'chan')
The draws below stay inside these ranges and needn't reach their ends.
All inputs are finite; a program needn't handle non-finite values.
Results may differ from the reference program's by a relative error of at most 0.008.
Values may be sent and summed in bfloat16 or wider, within the bound.
A program may use at most 64 MiB of HBM per device.

```python
import math
import jax
import jax.numpy as jnp
from jax import lax

D = 4096
MODES = 16
TOK_DEV = 256
SEQ = 16384
N_CHAN = 8


def block_levels(stream_key, dims, split, low, top_value):
    def one(axis_at, shards_of):
        steps = jax.random.uniform(jax.random.fold_in(jax.random.fold_in(stream_key, 6), axis_at), (shards_of,), jnp.float32, low / len(split), top_value / len(split))
        return jnp.repeat(jnp.exp(steps), dims[axis_at] // shards_of).reshape((-1,) + (1,) * (len(dims) - axis_at - 1))

    gain = one(*split[0])
    for cut in split[1:]:
        gain = gain * one(*cut)
    return gain


def normal_values(stream_key, shape, scale, most, cuts=(), kind=jnp.bfloat16):
    entries = scale * jax.random.normal(stream_key, shape, jnp.float32)
    if cuts:
        entries = entries * block_levels(stream_key, shape, cuts, -0.22, 0.18)
    return jnp.clip(entries, -most, most).astype(kind)


def setup_inputs(seed: int = 0) -> dict:
    seeds = jax.random.split(jax.random.key(seed), 7)
    return {
        "tokens": normal_values(seeds[0], (SEQ, D), 1.0, 6.0, ((0, 64), (1, 8))),
        "w_in": normal_values(seeds[1], (D, 3, D), D ** -0.5, 0.09375, ((0, 64), (2, 8))),
        "short_taps": normal_values(seeds[2], (3, 3, D), 0.6, 3.0, ((2, 8),), jnp.float32),
        "residues": normal_values(seeds[3], (MODES, D), (4 * MODES * TOK_DEV) ** -0.5, 0.046875, ((1, 8),), jnp.float32),
        "poles": jnp.clip(jnp.exp(math.log(512.0) - 7.4422974 * jax.random.uniform(seeds[4], (MODES, D), jnp.float32) ** block_levels(seeds[4], (MODES, D), ((1, 8),), -0.2, 0.2)), 0.3, 512.0),
        "skip_gain": jnp.clip(0.5 + 1.0 * jax.random.uniform(seeds[5], (D,), jnp.float32) ** block_levels(seeds[5], (D,), ((0, 8),), -0.2, 0.2), 0.5, 1.5),
    }


def modal_filter(count, length, residues, poles):
    scaled = jnp.arange(count, dtype=jnp.float32) / length
    total = jnp.zeros((count, residues.shape[1]), jnp.float32)
    for mode in range(residues.shape[0]):
        total = total + residues[mode][None, :] * jnp.exp(-poles[mode][None, :] * scaled[:, None])
    return total


def long_conv(filter_taps, gated):
    nfft = 2 * SEQ
    block = D // N_CHAN
    groups = D // block

    def one_group(pair):
        taps_part, data_part = pair
        spectrum = jnp.fft.rfft(taps_part, nfft, axis=0) * jnp.fft.rfft(data_part, nfft, axis=0)
        return jnp.fft.irfft(spectrum, nfft, axis=0)[:SEQ]

    taps_groups = filter_taps.reshape(SEQ, groups, block).transpose(1, 0, 2)
    data_groups = gated.astype(jnp.float32).reshape(SEQ, groups, block).transpose(1, 0, 2)
    result = lax.map(one_group, (taps_groups, data_groups))
    return result.transpose(1, 0, 2).reshape(SEQ, D)


def reference(tokens, w_in, short_taps, residues, poles, skip_gain):
    projected = jnp.dot(tokens, w_in.reshape(D, 3 * D), preferred_element_type=jnp.float32)
    projected = projected.astype(jnp.bfloat16).reshape(SEQ, 3, D)
    previous = jnp.zeros((2, 3, D), jnp.bfloat16)
    extended = jnp.concatenate([previous, projected], axis=0).astype(jnp.float32)
    smoothed = short_taps[0] * extended[2:] + short_taps[1] * extended[1:-1] + short_taps[2] * extended[:-2]
    query = smoothed[:, 0]
    gated = (smoothed[:, 1] * smoothed[:, 2]).astype(jnp.bfloat16)
    filter_taps = modal_filter(SEQ, SEQ, residues, poles)
    convolved = long_conv(filter_taps, gated)
    return (query * (convolved + skip_gain * gated.astype(jnp.float32))).astype(jnp.bfloat16)
```

```python
import jax
import jax.numpy as jnp
from jax import lax
from jax.experimental import pallas as pl
from jax.experimental.pallas import tpu as pltpu
from jax.sharding import PartitionSpec as P

MESH = pl.DeviceIdType.MESH
F32, BF16 = jnp.float32, jnp.bfloat16
ROWS = 256
CH = 512
DEPTH = 64
MODES = 16
SEQ = 16384.0
SUBS = 8
STEPS = ROWS // SUBS
COPIES = 112


def rounded(value):
    return value.astype(BF16).astype(F32)


def kernel(
    tok, w, taps, res, poles, skip, out,
    wbuf, xbuf, acc, legs, gbuf, ybuf, qbuf, obuf, ends, prefix, decay, tail_w, head_w, powers,
    state, sib_state, c_msg, y_in, r_msg, x_in, z_msg, z_in, k_msg, k_in, carry, halo_out, halo_in,
    send, recv, loc,
):
    s, c = lax.axis_index("seq"), lax.axis_index("chan")
    k, zh = lax.rem(s, 2), lax.rem(lax.div(s, 2), 2)
    y, x = lax.rem(lax.div(s, 4), 4), lax.div(s, 16)

    def at(px=x, py=y, pzh=zh, pk=k, pc=c):
        return (((px * 4 + py) * 2 + pzh) * 2 + pk, pc)

    def xs(d):
        return lax.rem(x + d + 4, 4)

    def ys(d):
        return lax.rem(y + d + 4, 4)

    over = lax.div(c + 4, 8)
    far_c = lax.rem(c + 4, 8)
    z_up = at(pzh=lax.rem(zh + over, 2), pc=far_c)
    z_dn = at(pzh=lax.rem(zh + over + 1, 2), pc=far_c)
    sibling = at(pk=1 - k)
    opposite = at(pzh=1 - zh)
    up, dn = lax.rem(c + 1, 8), lax.rem(c + 7, 8)
    after, before = (lax.rem(s + 1, 64), c), (lax.rem(s + 63, 64), c)

    barrier = pltpu.get_barrier_semaphore()
    partners = [sibling, opposite, z_up, z_dn, (s, up), (s, dn), after, before]
    for d in (1, 2, 3):
        partners += [at(px=xs(d)), at(py=ys(d))]
    for partner in partners:
        pl.semaphore_signal(barrier, inc=1, device_id=partner, device_id_type=MESH)
    pl.semaphore_wait(barrier, len(partners))

    sent = []

    def start(src, dst, to, cond=None):
        i = len(sent)
        copy = pltpu.make_async_remote_copy(
            src_ref=src, dst_ref=dst, send_sem=send.at[i], recv_sem=recv.at[i],
            device_id=to, device_id_type=MESH,
        )
        if cond is None:
            copy.start()
        else:
            pl.when(cond)(lambda: copy.start())
        sent.append((copy, cond))
        return copy

    chain = {}

    def tok_send(j, h):
        rows = pl.ds(h * 128, 128)
        low, high = lax.rem(c - j + 9, 8), lax.rem(c + j - 1, 8)
        for way, block, to, cond in (
            (0, low, up, (c < 7) & (c >= j - 1)),
            (1, high, dn, (c > 0) & (c + j <= 8)),
        ):
            src = tok.at[rows] if j == 1 else xbuf.at[block, rows]
            chain[j, h, way] = start(src, xbuf.at[block, rows], (s, to), cond)

    def tok_step(j, h):
        pl.when(c >= j)(lambda: chain[j, h, 0].wait_recv())
        pl.when(c + j <= 7)(lambda: chain[j, h, 1].wait_recv())
        if j < 7:
            tok_send(j + 1, h)

    def one(which, d, zz, rows):
        px, py = (xs(d), y) if which == "x" else (x, ys(d))
        return wbuf.at[px, py, zz, k, rows]

    def line(which, d, zz, rows):
        if which == "x":
            return wbuf.at[xs(d), pl.ds(0, 4), zz, k, rows]
        return wbuf.at[pl.ds(0, 4), ys(d), zz, k, rows]

    def to(which, d):
        return at(px=xs(d)) if which == "x" else at(py=ys(d))

    ORDER = (("x", "y", 0), ("y", "x", 32))

    class Gather:
        def __init__(self, zz, own):
            self.zz = zz
            self.sib = []
            self.near = {}
            for first, _, r in ORDER:
                rows = pl.ds(r, 32)
                src = w.at[rows] if own else one(first, 0, zz, rows)
                for d in (1, -1):
                    self.near[first, d] = start(src, one(first, 0, zz, rows), to(first, d))

        def pass_on(self):
            self.far = []
            for first, _, r in ORDER:
                for d in (1, -1):
                    rows = pl.ds(r + (0 if d == 1 else 16), 16)
                    self.near[first, d].wait_recv()
                    self.far.append(start(one(first, -d, self.zz, rows), one(first, -d, self.zz, rows), to(first, d)))

        def turn(self):
            for copy in self.far:
                copy.wait_recv()
            self.near2 = {}
            for _, second, r in ORDER:
                ref = line(second, 0, self.zz, pl.ds(r, 32))
                for d in (1, -1):
                    self.near2[second, d] = start(ref, ref, to(second, d))
            for _, second, r in ORDER:
                ref = line(second, 0, self.zz, pl.ds(r, 32))
                self.sib.append(start(ref, ref, sibling))

        def pass_on2(self):
            self.far2 = []
            for _, second, r in ORDER:
                for d in (1, -1):
                    rows = pl.ds(r + (0 if d == 1 else 16), 16)
                    self.near2[second, d].wait_recv()
                    ref = line(second, -d, self.zz, rows)
                    self.far2.append(start(ref, ref, to(second, d)))
            for _, second, r in ORDER:
                for d in (1, -1):
                    ref = line(second, d, self.zz, pl.ds(r, 32))
                    self.sib.append(start(ref, ref, sibling))

        def finish(self):
            for copy in self.far2:
                copy.wait_recv()
            for _, second, r in ORDER:
                ref = line(second, 2, self.zz, pl.ds(r, 32))
                self.sib.append(start(ref, ref, sibling))

        def wait_sibling(self):
            for copy in self.sib:
                copy.wait_recv()

    leg_a = start(w.at[pl.ds(0, 32)], legs.at[0], z_up)
    leg_b = start(w.at[pl.ds(32, 32)], legs.at[1], z_dn)
    tok_send(1, 0)
    tok_send(1, 1)
    mine = Gather(zh, True)
    keep_w = pltpu.make_async_copy(w, wbuf.at[x, y, zh, k], loc.at[0])
    keep_x = pltpu.make_async_copy(tok, xbuf.at[c], loc.at[1])
    keep_w.start()
    keep_x.start()

    def tables():
        acc[...] = jnp.zeros_like(acc)
        rate = poles[...] * (-1.0 / SEQ)
        decay[...] = jnp.exp(rate)
        powers[0] = jnp.exp(rate * ROWS)
        powers[1] = jnp.exp(rate * (2.0 * ROWS))
        powers[2] = jnp.exp(rate * (4.0 * ROWS))
        powers[3] = jnp.exp(rate * (16.0 * ROWS))
        powers[4] = jnp.exp(rate * ((4.0 * ROWS) * y.astype(F32)))
        powers[5] = jnp.exp(rate * (STEPS - 1.0))
        powers[6] = jnp.exp(rate * (STEPS - 2.0))
        sub = lax.broadcasted_iota(jnp.int32, (SUBS, CH), 0).astype(F32)
        for n in range(MODES):
            r = poles[n : n + 1, :] * (-STEPS / SEQ)
            head_w[n] = jnp.exp(r * sub)
            tail_w[n] = jnp.exp(r * (SUBS - 1.0 - sub))

    tok_step(1, 0)
    mine.pass_on()
    tok_step(1, 1)
    keep_w.wait()
    mine.turn()
    tables()
    tok_step(2, 0)
    leg_a.wait_recv()
    leg_c = start(legs.at[0], wbuf.at[x, y, 1 - z_up_zh(zh, over), k, pl.ds(0, 32)], z_up)
    leg_b.wait_recv()
    leg_d = start(legs.at[1], wbuf.at[x, y, z_up_zh(zh, over), k, pl.ds(32, 32)], z_dn)
    tok_step(2, 1)
    mine.pass_on2()
    tok_step(3, 0)
    tok_step(3, 1)
    mine.finish()
    leg_c.wait_recv()
    leg_d.wait_recv()
    theirs = Gather(1 - zh, False)
    tok_step(4, 0)
    theirs.pass_on()
    tok_step(4, 1)
    theirs.turn()
    tok_step(5, 0)
    tok_step(5, 1)
    theirs.pass_on2()
    tok_step(6, 0)
    mine.wait_sibling()
    tok_step(6, 1)
    theirs.finish()
    keep_x.wait()
    theirs.wait_sibling()

    def dot_chunk(cc):
        px, py = lax.div(cc, 2), lax.rem(cc, 2) * 2
        for g in range(3):
            cols = pl.ds(g * CH, CH)
            part = wbuf[px, pl.ds(py, 2), :, :, :, cols].reshape(CH, CH)
            dot = jnp.dot(xbuf[cc], part, preferred_element_type=F32)
            for lg in range(4):
                acc[4 * g + lg, 8:, :] += dot[:, lg * 128 : (lg + 1) * 128]

    def dots(lo, hi):
        def body(j, _):
            pl.when(c >= j)(lambda: dot_chunk(lax.rem(c - j + 8, 8)))
            pl.when((j > 0) & (c + j <= 7))(lambda: dot_chunk(lax.rem(c + j, 8)))
            return 0

        lax.fori_loop(lo, hi, body, 0)

    dots(0, 7)
    tok_step(7, 0)
    tok_step(7, 1)
    dots(7, 8)

    for r in range(2):
        for i in range(12):
            row, cols = 3 * r + i // 4, (i % 4) * 128
            halo_out[row : row + 1, cols : cols + 128] = rounded(acc[i, 6 + ROWS + r : 7 + ROWS + r, :])
    halo = start(halo_out, halo_in, after, s < 63)

    def lanes(lg):
        return pl.ds(lg * 128, 128)

    def rows_of(ref, lg):
        return [jnp.broadcast_to(ref[n : n + 1, lanes(lg)], (SUBS, 128)) for n in range(MODES)]

    def filter_of(g, lg):
        t = [jnp.broadcast_to(taps[i, g : g + 1, lanes(lg)], (SUBS, 128)) for i in range(3)]

        def load(first):
            return rounded(acc[4 * g + lg, pl.ds(first, SUBS, stride=STEPS), :])

        return lambda p0, p1, p2: t[0] * p0 + t[1] * p1 + t[2] * p2, load

    def gate(fk, fv, k3, v3):
        return rounded(fk(*k3) * fv(*v3))

    def pass_a(lg):
        (fk, lk), (fv, lv) = filter_of(1, lg), filter_of(2, lg)
        a = rows_of(decay, lg)

        def body(i, held):
            k1, k2, v1, v2, st = held
            k0, v0 = lk(8 + i), lv(8 + i)
            g = gate(fk, fv, (k0, k1, k2), (v0, v1, v2))
            gbuf[i, :, lanes(lg)] = g
            return k0, k1, v0, v1, tuple(a[n] * st[n] + g for n in range(MODES))

        zero = tuple(jnp.zeros((SUBS, 128), F32) for _ in range(MODES))
        held = lax.fori_loop(0, STEPS, body, (lk(7), lk(6), lv(7), lv(6), zero), unroll=4)
        for n in range(MODES):
            ends[n, :, lanes(lg)] = held[4][n]

    for lg in range(4):
        pass_a(lg)

    @pl.when(s > 0)
    def _():
        halo.wait_recv()
        for r in range(2):
            for i in range(12):
                row, cols = 3 * r + i // 4, (i % 4) * 128
                acc[i, 6 + r : 7 + r, :] = halo_in[row : row + 1, cols : cols + 128]

    for lg in range(4):
        (fk, lk), (fv, lv) = filter_of(1, lg), filter_of(2, lg)
        pk, pv = [lk(6 + i) for i in range(4)], [lv(6 + i) for i in range(4)]
        g0 = gate(fk, fv, pk[2::-1], pv[2::-1])
        g1 = gate(fk, fv, pk[3:0:-1], pv[3:0:-1])
        d0, d1 = g0 - gbuf[0, :, lanes(lg)], g1 - gbuf[1, :, lanes(lg)]
        gbuf[0, :, lanes(lg)] = g0
        gbuf[1, :, lanes(lg)] = g1
        for n in range(MODES):
            end = ends[n, :, lanes(lg)] + powers[5, n : n + 1, lanes(lg)] * d0 + powers[6, n : n + 1, lanes(lg)] * d1
            ends[n, :, lanes(lg)] = end
            state[n : n + 1, lanes(lg)] = jnp.sum(tail_w[n, :, lanes(lg)] * end, axis=0, keepdims=True)

    def pass_b(lg):
        fq, lq = filter_of(0, lg)
        a, r = rows_of(decay, lg), rows_of(res, lg)
        gain = jnp.broadcast_to(skip[0:1, lanes(lg)], (SUBS, 128))

        def body(i, held):
            q1, q2, st = held
            q0 = lq(8 + i)
            qbuf[i, :, lanes(lg)] = fq(q0, q1, q2)
            g = gbuf[i, :, lanes(lg)]
            st = tuple(a[n] * st[n] + g for n in range(MODES))
            ybuf[i, :, lanes(lg)] = total([r[n] * st[n] for n in range(MODES)] + [gain * g])
            return q0, q1, st

        zero = tuple(jnp.zeros((SUBS, 128), F32) for _ in range(MODES))
        lax.fori_loop(0, STEPS, body, (lq(7), lq(6), zero), unroll=2)
        sub = lax.broadcasted_iota(jnp.int32, (SUBS, 128), 0)

        def down(value, by):
            return jnp.where(sub >= by, pltpu.roll(value, by, 0), 0.0)

        for n in range(MODES):
            v = down(ends[n, :, lanes(lg)], 1)
            for by in (1, 2, 4):
                v = v + head_w[n, by : by + 1, lanes(lg)] * down(v, by)
            prefix[n, :, lanes(lg)] = v

    half = pl.ds(pl.multiple_of(k * 256, 256), 256)
    other = pl.ds(pl.multiple_of((1 - k) * 256, 256), 256)
    first = start(state, sib_state, sibling)
    pass_b(0)
    first.wait_recv()
    own, sib = state[:, half], sib_state[:, half]
    chip = powers[0, :, half] * jnp.where(k == 0, own, sib) + jnp.where(k == 0, sib, own)
    c_msg[...] = chip
    y_in[y] = chip
    level = [start(c_msg, y_in.at[y], at(py=ys(d))) for d in (1, 2, 3)]
    pass_b(1)
    for copy in level:
        copy.wait_recv()
    d4 = powers[2, :, half]
    row, early = jnp.zeros_like(chip), jnp.zeros_like(chip)
    for i in range(4):
        got = y_in[i]
        row = row * d4 + got
        early = jnp.where(i < y, early * d4 + got, early)
    r_msg[...] = row
    x_in[x] = row
    level = [start(r_msg, x_in.at[x], at(px=xs(d))) for d in (1, 2, 3)]
    pass_b(2)
    for copy in level:
        copy.wait_recv()
    d16, lead = powers[3, :, half], jnp.zeros_like(chip)
    for i in range(4):
        lead = jnp.where(i < x, lead * d16 + x_in[i], lead)
    plane = early + powers[4, :, half] * lead
    z_msg[...] = jnp.where(zh == 0, d4 * plane + chip, plane)
    level = start(z_msg, z_in, opposite)
    pass_b(3)
    level.wait_recv()
    into = powers[1, :, half] * plane + z_in[...]
    k_msg[...] = into
    level = start(k_msg, k_in, sibling)
    carry[:, half] = into
    level.wait_recv()
    carry[:, other] = k_in[...]
    carry[...] = jnp.where(k == 0, carry[...], powers[0] * carry[...] + sib_state[...])

    def pass_c(lg):
        a, r = rows_of(decay, lg), rows_of(res, lg)
        ws = tuple(
            r[n] * (prefix[n, :, lanes(lg)] + head_w[n, :, lanes(lg)] * carry[n : n + 1, lanes(lg)])
            for n in range(MODES)
        )

        def body(i, ws):
            ws = tuple(a[n] * ws[n] for n in range(MODES))
            value = ybuf[i, :, lanes(lg)] + total(list(ws))
            obuf[lg, pl.ds(i, SUBS, stride=STEPS), :] = qbuf[i, :, lanes(lg)] * value
            return ws

        lax.fori_loop(0, STEPS, body, ws, unroll=4)
        out[:, lanes(lg)] = obuf[lg].astype(BF16)

    for lg in range(4):
        pass_c(lg)

    for copy, cond in sent:
        if cond is None:
            copy.wait_send()
        else:
            pl.when(cond)(lambda copy=copy: copy.wait_send())


def z_up_zh(zh, over):
    return lax.rem(zh + over, 2)


def total(values):
    while len(values) > 1:
        values = [a + b for a, b in zip(values[::2], values[1::2])] + values[len(values) & ~1 :]
    return values[0]


def local(tokens, w_in, short_taps, residues, poles, skip_gain):
    vmem = pl.BlockSpec(memory_space=pltpu.VMEM)
    block = pltpu.VMEM((STEPS, SUBS, CH), F32)
    table = pltpu.VMEM((MODES, SUBS, CH), F32)
    full, part = pltpu.VMEM((MODES, CH), F32), pltpu.VMEM((MODES, CH // 2), F32)
    parts4 = pltpu.VMEM((4, MODES, CH // 2), F32)
    halo = pltpu.VMEM((8, CH), F32)
    return pl.pallas_call(
        kernel,
        out_shape=jax.ShapeDtypeStruct((ROWS, CH), BF16),
        in_specs=[vmem] * 6,
        out_specs=vmem,
        scratch_shapes=[
            pltpu.VMEM((4, 4, 2, 2, DEPTH, 3 * CH), BF16),
            pltpu.VMEM((8, ROWS, CH), BF16),
            pltpu.VMEM((12, 8 + ROWS, 128), F32),
            pltpu.VMEM((2, DEPTH // 2, 3 * CH), BF16),
            block, block, block,
            pltpu.VMEM((4, ROWS, 128), F32),
            table, table, full, table, table,
            pltpu.VMEM((7, MODES, CH), F32),
            full, full, part, parts4, part, parts4, part, part, part, part, full, halo, halo,
            pltpu.SemaphoreType.DMA((COPIES,)),
            pltpu.SemaphoreType.DMA((COPIES,)),
            pltpu.SemaphoreType.DMA((2,)),
        ],
        compiler_params=pltpu.CompilerParams(
            collective_id=0, has_side_effects=True, vmem_limit_bytes=40 * 1024 * 1024
        ),
    )(tokens, w_in.reshape(DEPTH, 3 * CH), short_taps, residues, poles, skip_gain.reshape(1, CH))


def solution(mesh):
    placed = (
        P("seq", "chan"),
        P("seq", None, "chan"),
        P(None, None, "chan"),
        P(None, "chan"),
        P(None, "chan"),
        P("chan"),
    )
    return jax.shard_map(
        local, mesh=mesh, in_specs=placed, out_specs=P("seq", "chan"), check_vma=False
    )
```

```python
import jax
import jax.numpy as jnp
from jax import lax
from jax.experimental import pallas as pl
from jax.experimental.pallas import tpu as pltpu
from jax.sharding import PartitionSpec as P

MESH = pl.DeviceIdType.MESH
F32, BF16 = jnp.float32, jnp.bfloat16
ROWS = 256
CH = 512
DEPTH = 64
MODES = 16
SEQ = 16384.0
SUBS = 8
STEPS = ROWS // SUBS
TOP = 16
COPIES = 176


def rounded(value):
    return value.astype(BF16).astype(F32)


def kernel(
    tok, w, taps, res, poles, skip, out,
    wbuf, xbuf, acc, legs, gbuf, ybuf, qbuf, obuf, ends, prefix, decay, tail_w, head_w, powers,
    state, sib_state, c_msg, y_in, r_msg, x_in, z_msg, z_in, k_msg, k_in, carry, packed, last_out, last_in, last,
    send, recv, loc,
):
    s, c = lax.axis_index("seq"), lax.axis_index("chan")
    k, zh = lax.rem(s, 2), lax.rem(lax.div(s, 2), 2)
    y, x = lax.rem(lax.div(s, 4), 4), lax.div(s, 16)

    def at(px=x, py=y, pzh=zh, pk=k, pc=c):
        return (((px * 4 + py) * 2 + pzh) * 2 + pk, pc)

    def xs(d):
        return lax.rem(x + d + 4, 4)

    def ys(d):
        return lax.rem(y + d + 4, 4)

    over = lax.div(c + 4, 8)
    far_c = lax.rem(c + 4, 8)
    z_up = at(pzh=lax.rem(zh + over, 2), pc=far_c)
    z_dn = at(pzh=lax.rem(zh + over + 1, 2), pc=far_c)
    sibling = at(pk=1 - k)
    opposite = at(pzh=1 - zh)
    up, dn = lax.rem(c + 1, 8), lax.rem(c + 7, 8)
    after, before = (lax.rem(s + 1, 64), c), (lax.rem(s + 63, 64), c)

    barrier = pltpu.get_barrier_semaphore()
    partners = [sibling, opposite, z_up, z_dn, (s, up), (s, dn), after, before]
    for d in (1, 2, 3):
        partners += [at(px=xs(d)), at(py=ys(d))]
    for partner in partners:
        pl.semaphore_signal(barrier, inc=1, device_id=partner, device_id_type=MESH)
    pl.semaphore_wait(barrier, len(partners))

    sent = []

    def start(src, dst, to, cond=None):
        i = len(sent)
        copy = pltpu.make_async_remote_copy(
            src_ref=src, dst_ref=dst, send_sem=send.at[i], recv_sem=recv.at[i],
            device_id=to, device_id_type=MESH,
        )
        if cond is None:
            copy.start()
        else:
            pl.when(cond)(lambda: copy.start())
        sent.append((copy, cond))
        return copy

    chain = {}

    def pass_along(j, key, ref):
        low, high = lax.rem(c - j + 9, 8), lax.rem(c + j - 1, 8)
        for way, block, to, cond in (
            (0, low, up, (c < 7) & (c >= j - 1)),
            (1, high, dn, (c > 0) & (c + j <= 8)),
        ):
            chain[j, key, way] = start(ref(block), ref(block), (s, to), cond)

    def arrive(j, key):
        pl.when(c >= j)(lambda: chain[j, key, 0].wait_recv())
        pl.when(c + j <= 7)(lambda: chain[j, key, 1].wait_recv())

    def tok_send(j, h):
        pass_along(j, h, lambda block: xbuf.at[block, pl.ds(2 * h, 2)])

    def last_send(j):
        pass_along(j, "last", lambda block: last.at[block])

    def tok_step(j, h):
        arrive(j, h)
        if j < 7:
            tok_send(j + 1, h)

    def last_step(j):
        arrive(j, "last")
        if j < 7:
            last_send(j + 1)

    def one(which, d, zz, rows):
        px, py = (xs(d), y) if which == "x" else (x, ys(d))
        return wbuf.at[px, py, zz, k, rows]

    def line(which, d, zz, rows):
        if which == "x":
            return wbuf.at[xs(d), pl.ds(0, 4), zz, k, rows]
        return wbuf.at[pl.ds(0, 4), ys(d), zz, k, rows]

    def to(which, d):
        return at(px=xs(d)) if which == "x" else at(py=ys(d))

    ORDER = (("x", "y", 0), ("y", "x", 32))

    class Gather:
        def __init__(self, zz, own):
            self.zz, self.own = zz, own
            self.sib, self.near, self.far, self.turned, self.passed = [], {}, [], {}, []
            for first, _, r in ORDER:
                rows = pl.ds(r, 32)
                src = w.at[rows] if own else one(first, 0, zz, rows)
                for d in (1, -1):
                    self.near[first, d] = start(src, one(first, 0, zz, rows), to(first, d))
            for first, second, r in ORDER:
                self.turn(first, second, r, 0)

        def turn(self, first, second, r, p):
            ref = one(first, p, self.zz, pl.ds(r, 32))
            src = w.at[pl.ds(r, 32)] if self.own and p == 0 else ref
            for d in (1, -1):
                self.turned[second, p, d] = start(src, ref, to(second, d))

        def half(self, r, d):
            return pl.ds(r + (0 if d == 1 else 16), 16)

        def pass_turned(self, first, second, r, p):
            for d in (1, -1):
                self.turned[second, p, d].wait_recv()
                px, py = (xs(p), ys(-d)) if second == "y" else (xs(-d), ys(p))
                ref = wbuf.at[px, py, self.zz, k, self.half(r, d)]
                self.passed.append(start(ref, ref, to(second, d)))

        def to_sibling(self, second, d, r):
            ref = line(second, d, self.zz, pl.ds(r, 32))
            self.sib.append(start(ref, ref, sibling))

        def step1(self):
            for first, second, r in ORDER:
                for d in (1, -1):
                    self.near[first, d].wait_recv()
                    ref = one(first, -d, self.zz, self.half(r, d))
                    self.far.append(start(ref, ref, to(first, d)))
                    self.turn(first, second, r, -d)
            for first, second, r in ORDER:
                self.pass_turned(first, second, r, 0)

        def step2(self):
            for copy in self.far:
                copy.wait_recv()
            for first, second, r in ORDER:
                self.turn(first, second, r, 2)
            for first, second, r in ORDER:
                self.to_sibling(second, 0, r)
            for p in (1, -1):
                for first, second, r in ORDER:
                    self.pass_turned(first, second, r, p)

        def step3(self):
            for first, second, r in ORDER:
                self.pass_turned(first, second, r, 2)
            for _, second, r in ORDER:
                for d in (1, -1):
                    self.to_sibling(second, d, r)

        def step4(self):
            for copy in self.passed:
                copy.wait_recv()
            for _, second, r in ORDER:
                self.to_sibling(second, 2, r)

        def wait_sibling(self):
            for copy in self.sib:
                copy.wait_recv()

    def leg(way, r):
        return start(w.at[pl.ds(32 * way + r, 16)], legs.at[way, pl.ds(r, 16)], z_dn if way else z_up)

    def next_leg(way, r):
        zz = lax.rem(zh + over, 2)
        dst = wbuf.at[x, y, zz if way else 1 - zz, k, pl.ds(32 * way + r, 16)]
        return start(legs.at[way, pl.ds(r, 16)], dst, z_dn if way else z_up)

    leg1 = [leg(way, r) for r in (0, 16) for way in (0, 1)]
    mine = Gather(zh, True)
    keep_w = pltpu.make_async_copy(w, wbuf.at[x, y, zh, k], loc.at[0])
    keep_w.start()
    packed[...] = jnp.zeros_like(packed)
    for j in range(4):
        xbuf[c, j] = tok[:, j * 128 : (j + 1) * 128]
        packed[2 * j : 2 * j + 2, :] = tok[ROWS - 16 :, j * 128 : (j + 1) * 128].astype(F32)[14:, :]
    last_out[...] = packed[...].astype(BF16)
    handed = start(last_out, last_in, after)

    def tables():
        acc[...] = jnp.zeros_like(acc)
        rate = poles[...] * (-1.0 / SEQ)
        decay[...] = jnp.exp(rate)
        powers[0] = jnp.exp(rate * ROWS)
        powers[1] = jnp.exp(rate * (2.0 * ROWS))
        powers[2] = jnp.exp(rate * (4.0 * ROWS))
        powers[3] = jnp.exp(rate * (16.0 * ROWS))
        powers[4] = jnp.exp(rate * ((4.0 * ROWS) * y.astype(F32)))
        sub = lax.broadcasted_iota(jnp.int32, (SUBS, CH), 0).astype(F32)
        for n in range(MODES):
            r = poles[n : n + 1, :] * (-STEPS / SEQ)
            head_w[n] = jnp.exp(r * sub)
            tail_w[n] = jnp.exp(r * (SUBS - 1.0 - sub))

    def add_dot(cc, left, right):
        for g in range(3):
            dot = jnp.dot(left, right(pl.ds(g * CH, CH)), preferred_element_type=F32)
            for lg in range(4):
                acc[4 * g + lg] += dot[:, lg * 128 : (lg + 1) * 128]

    row = lax.broadcasted_iota(jnp.int32, (TOP, 128), 0)

    def features(cc, j):
        top = jnp.where((row >= 2 * j) & (row < 2 * j + 2), last[cc].astype(F32), 0.0).astype(BF16)
        return jnp.concatenate([top, xbuf[cc, j]], axis=0)

    def dot_z(zz, cc):
        px, py = lax.div(cc, 2), lax.rem(cc, 2) * 2
        left = jnp.concatenate([features(cc, zz), features(cc, zz + 2)], axis=1)
        add_dot(cc, left, lambda cols: wbuf[px, pl.ds(py, 2), zz, :, :, cols].reshape(256, CH))

    def dot_y(p, cc):
        px, py = lax.div(cc, 2), lax.rem(cc, 2) * 2 + p
        left = jnp.concatenate([features(cc, 2 * p), features(cc, 2 * p + 1)], axis=1)
        add_dot(cc, left, lambda cols: wbuf[px, py, :, :, :, cols].reshape(256, CH))

    def dots(kind, which, lo, hi):
        def body(j, _):
            pl.when(c >= j)(lambda: kind(which, lax.rem(c - j + 8, 8)))
            pl.when((j > 0) & (c + j <= 7))(lambda: kind(which, lax.rem(c + j, 8)))
            return 0

        lax.fori_loop(lo, hi, body, 0)

    mine.step1()
    leg2 = []
    for copy, (r, way) in zip(leg1, ((0, 0), (0, 1), (16, 0), (16, 1))):
        copy.wait_recv()
        leg2.append(next_leg(way, r))
    tok_send(1, 0)
    tok_send(1, 1)
    keep_w.wait()
    mine.step2()
    tables()
    mine.step3()
    handed.wait_recv()
    last[c] = jnp.where(s > 0, last_in[...].astype(F32), 0.0).astype(BF16)
    last_send(1)
    tok_step(1, 0)
    for copy in leg2:
        copy.wait_recv()
    theirs = Gather(1 - zh, False)
    tok_step(1, 1)
    last_step(1)
    mine.step4()
    tok_step(2, 0)
    theirs.step1()
    tok_step(2, 1)
    last_step(2)
    mine.wait_sibling()
    dots(dot_z, zh, 0, 2)
    theirs.step2()
    tok_step(3, 0)
    tok_step(3, 1)
    last_step(3)
    theirs.step3()
    dots(dot_z, zh, 2, 4)
    tok_step(4, 0)
    tok_step(4, 1)
    last_step(4)
    theirs.step4()
    tok_step(5, 0)
    tok_step(5, 1)
    last_step(5)
    dots(dot_z, zh, 4, 6)
    theirs.wait_sibling()
    dots(dot_z, 1 - zh, 0, 6)
    tok_step(6, 0)
    tok_step(6, 1)
    last_step(6)
    dots(dot_z, zh, 6, 7)
    dots(dot_z, 1 - zh, 6, 7)
    tok_step(7, 0)
    last_step(7)
    dots(dot_y, 0, 7, 8)
    tok_step(7, 1)
    dots(dot_y, 1, 7, 8)
    for i in range(12):
        for r in range(2):
            two = [acc[i, 2 * j + r : 2 * j + r + 1, :] for j in range(4)]
            acc[i, TOP - 2 + r : TOP - 1 + r, :] = total(two)

    def lanes(lg):
        return pl.ds(lg * 128, 128)

    def rows_of(ref, lg):
        return [jnp.broadcast_to(ref[n : n + 1, lanes(lg)], (SUBS, 128)) for n in range(MODES)]

    def filter_of(g, lg):
        t = [jnp.broadcast_to(taps[i, g : g + 1, lanes(lg)], (SUBS, 128)) for i in range(3)]

        def load(first):
            return rounded(acc[4 * g + lg, pl.ds(first, SUBS, stride=STEPS), :])

        return lambda p0, p1, p2: t[0] * p0 + t[1] * p1 + t[2] * p2, load

    def gate(fk, fv, k3, v3):
        return rounded(fk(*k3) * fv(*v3))

    def pass_a(lg):
        (fk, lk), (fv, lv) = filter_of(1, lg), filter_of(2, lg)
        a = rows_of(decay, lg)

        def body(i, held):
            k1, k2, v1, v2, st = held
            k0, v0 = lk(TOP + i), lv(TOP + i)
            g = gate(fk, fv, (k0, k1, k2), (v0, v1, v2))
            gbuf[i, :, lanes(lg)] = g
            return k0, k1, v0, v1, tuple(a[n] * st[n] + g for n in range(MODES))

        zero = tuple(jnp.zeros((SUBS, 128), F32) for _ in range(MODES))
        held = lax.fori_loop(0, STEPS, body, (lk(TOP - 1), lk(TOP - 2), lv(TOP - 1), lv(TOP - 2), zero), unroll=4)
        for n in range(MODES):
            ends[n, :, lanes(lg)] = held[4][n]
            state[n : n + 1, lanes(lg)] = jnp.sum(tail_w[n, :, lanes(lg)] * held[4][n], axis=0, keepdims=True)

    for lg in range(4):
        pass_a(lg)

    def pass_b(lg):
        fq, lq = filter_of(0, lg)
        a, r = rows_of(decay, lg), rows_of(res, lg)
        gain = jnp.broadcast_to(skip[0:1, lanes(lg)], (SUBS, 128))

        def body(i, held):
            q1, q2, st = held
            q0 = lq(TOP + i)
            qbuf[i, :, lanes(lg)] = fq(q0, q1, q2)
            g = gbuf[i, :, lanes(lg)]
            st = tuple(a[n] * st[n] + g for n in range(MODES))
            ybuf[i, :, lanes(lg)] = total([r[n] * st[n] for n in range(MODES)] + [gain * g])
            return q0, q1, st

        zero = tuple(jnp.zeros((SUBS, 128), F32) for _ in range(MODES))
        lax.fori_loop(0, STEPS, body, (lq(TOP - 1), lq(TOP - 2), zero), unroll=2)
        sub = lax.broadcasted_iota(jnp.int32, (SUBS, 128), 0)

        def down(value, by):
            return jnp.where(sub >= by, pltpu.roll(value, by, 0), 0.0)

        for n in range(MODES):
            v = down(ends[n, :, lanes(lg)], 1)
            for by in (1, 2, 4):
                v = v + head_w[n, by : by + 1, lanes(lg)] * down(v, by)
            prefix[n, :, lanes(lg)] = v

    half = pl.ds(pl.multiple_of(k * 256, 256), 256)
    other = pl.ds(pl.multiple_of((1 - k) * 256, 256), 256)
    first = start(state, sib_state, sibling)
    pass_b(0)
    first.wait_recv()
    own, sib = state[:, half], sib_state[:, half]
    chip = powers[0, :, half] * jnp.where(k == 0, own, sib) + jnp.where(k == 0, sib, own)
    c_msg[...] = chip
    y_in[y] = chip
    level = [start(c_msg, y_in.at[y], at(py=ys(d))) for d in (1, 2, 3)]
    pass_b(1)
    for copy in level:
        copy.wait_recv()
    d4 = powers[2, :, half]
    row, early = jnp.zeros_like(chip), jnp.zeros_like(chip)
    for i in range(4):
        got = y_in[i]
        row = row * d4 + got
        early = jnp.where(i < y, early * d4 + got, early)
    r_msg[...] = row
    x_in[x] = row
    level = [start(r_msg, x_in.at[x], at(px=xs(d))) for d in (1, 2, 3)]
    pass_b(2)
    for copy in level:
        copy.wait_recv()
    d16, lead = powers[3, :, half], jnp.zeros_like(chip)
    for i in range(4):
        lead = jnp.where(i < x, lead * d16 + x_in[i], lead)
    plane = early + powers[4, :, half] * lead
    z_msg[...] = jnp.where(zh == 0, d4 * plane + chip, plane)
    level = start(z_msg, z_in, opposite)
    pass_b(3)
    level.wait_recv()
    into = powers[1, :, half] * plane + z_in[...]
    k_msg[...] = into
    level = start(k_msg, k_in, sibling)
    carry[:, half] = into
    level.wait_recv()
    carry[:, other] = k_in[...]
    carry[...] = jnp.where(k == 0, carry[...], powers[0] * carry[...] + sib_state[...])

    def pass_c(lg):
        a, r = rows_of(decay, lg), rows_of(res, lg)
        ws = tuple(
            r[n] * (prefix[n, :, lanes(lg)] + head_w[n, :, lanes(lg)] * carry[n : n + 1, lanes(lg)])
            for n in range(MODES)
        )

        def body(i, ws):
            ws = tuple(a[n] * ws[n] for n in range(MODES))
            value = ybuf[i, :, lanes(lg)] + total(list(ws))
            obuf[lg, pl.ds(i, SUBS, stride=STEPS), :] = qbuf[i, :, lanes(lg)] * value
            return ws

        lax.fori_loop(0, STEPS, body, ws, unroll=4)
        out[:, lanes(lg)] = obuf[lg].astype(BF16)

    for lg in range(4):
        pass_c(lg)

    for copy, cond in sent:
        if cond is None:
            copy.wait_send()
        else:
            pl.when(cond)(lambda copy=copy: copy.wait_send())


def total(values):
    while len(values) > 1:
        values = [a + b for a, b in zip(values[::2], values[1::2])] + values[len(values) & ~1 :]
    return values[0]


def local(tokens, w_in, short_taps, residues, poles, skip_gain):
    vmem = pl.BlockSpec(memory_space=pltpu.VMEM)
    block = pltpu.VMEM((STEPS, SUBS, CH), F32)
    table = pltpu.VMEM((MODES, SUBS, CH), F32)
    full, part = pltpu.VMEM((MODES, CH), F32), pltpu.VMEM((MODES, CH // 2), F32)
    parts4 = pltpu.VMEM((4, MODES, CH // 2), F32)
    last = pltpu.VMEM((16, 128), BF16)
    return pl.pallas_call(
        kernel,
        out_shape=jax.ShapeDtypeStruct((ROWS, CH), BF16),
        in_specs=[vmem] * 6,
        out_specs=vmem,
        scratch_shapes=[
            pltpu.VMEM((4, 4, 2, 2, DEPTH, 3 * CH), BF16),
            pltpu.VMEM((8, 4, ROWS, 128), BF16),
            pltpu.VMEM((12, TOP + ROWS, 128), F32),
            pltpu.VMEM((2, DEPTH // 2, 3 * CH), BF16),
            block, block, block,
            pltpu.VMEM((4, ROWS, 128), F32),
            table, table, full, table, table,
            pltpu.VMEM((5, MODES, CH), F32),
            full, full, part, parts4, part, parts4, part, part, part, part, full,
            pltpu.VMEM((16, 128), F32), last, last, pltpu.VMEM((8, 16, 128), BF16),
            pltpu.SemaphoreType.DMA((COPIES,)),
            pltpu.SemaphoreType.DMA((COPIES,)),
            pltpu.SemaphoreType.DMA((1,)),
        ],
        compiler_params=pltpu.CompilerParams(
            collective_id=0, has_side_effects=True, vmem_limit_bytes=40 * 1024 * 1024
        ),
    )(tokens, w_in.reshape(DEPTH, 3 * CH), short_taps, residues, poles, skip_gain.reshape(1, CH))


def solution(mesh):
    placed = (
        P("seq", "chan"),
        P("seq", None, "chan"),
        P(None, None, "chan"),
        P(None, "chan"),
        P(None, "chan"),
        P("chan"),
    )
    return jax.shard_map(
        local, mesh=mesh, in_specs=placed, out_specs=P("seq", "chan"), check_vma=False
    )
```

```python
import jax
import jax.numpy as jnp
from jax import lax
from jax.experimental import pallas as pl
from jax.experimental.pallas import tpu as pltpu
from jax.sharding import PartitionSpec as P

MESH = pl.DeviceIdType.MESH
F32, BF16 = jnp.float32, jnp.bfloat16
ROWS = 256
CH = 512
DEPTH = 64
MODES = 16
SEQ = 16384.0
SUBS = 8
STEPS = ROWS // SUBS
TOP = 16
COPIES = 176


def rounded(value):
    return value.astype(BF16).astype(F32)


def kernel(
    tok, w, taps, res, poles, skip, out,
    wbuf, xbuf, acc, legs, gbuf, ybuf, qbuf, obuf, ends, prefix, decay, tail_w, head_w, powers,
    state, sib_state, c_msg, y_in, z_msg, z_in, k_msg, k_in, carry, packed, last_out, last_in, last,
    send, recv, loc,
):
    s, c = lax.axis_index("seq"), lax.axis_index("chan")
    k, zh = lax.rem(s, 2), lax.rem(lax.div(s, 2), 2)
    y, x = lax.rem(lax.div(s, 4), 4), lax.div(s, 16)

    def at(px=x, py=y, pzh=zh, pk=k, pc=c):
        return (((px * 4 + py) * 2 + pzh) * 2 + pk, pc)

    def xs(d):
        return lax.rem(x + d + 4, 4)

    def ys(d):
        return lax.rem(y + d + 4, 4)

    over = lax.div(c + 4, 8)
    far_c = lax.rem(c + 4, 8)
    z_up = at(pzh=lax.rem(zh + over, 2), pc=far_c)
    z_dn = at(pzh=lax.rem(zh + over + 1, 2), pc=far_c)
    sibling = at(pk=1 - k)
    opposite = at(pzh=1 - zh)
    up, dn = lax.rem(c + 1, 8), lax.rem(c + 7, 8)
    after, before = (lax.rem(s + 1, 64), c), (lax.rem(s + 63, 64), c)

    barrier = pltpu.get_barrier_semaphore()
    partners = [sibling, opposite, z_up, z_dn, (s, up), (s, dn), after, before]
    steps = [(dx, dy) for dx in range(4) for dy in range(4) if dx or dy]
    partners += [at(px=xs(dx), py=ys(dy)) for dx, dy in steps]
    for partner in partners:
        pl.semaphore_signal(barrier, inc=1, device_id=partner, device_id_type=MESH)
    pl.semaphore_wait(barrier, len(partners))

    sent, done = [], []

    def start(src, dst, to, cond=None):
        i = len(sent)
        copy = pltpu.make_async_remote_copy(
            src_ref=src, dst_ref=dst, send_sem=send.at[i], recv_sem=recv.at[i],
            device_id=to, device_id_type=MESH,
        )
        if cond is None:
            copy.start()
        else:
            pl.when(cond)(lambda: copy.start())
        sent.append((copy, cond))
        return copy

    def drain():
        for copy, cond in sent[len(done) :]:
            if cond is None:
                copy.wait_send()
            else:
                pl.when(cond)(lambda copy=copy: copy.wait_send())
            done.append(copy)

    chain = {}

    def pass_along(j, key, ref):
        low, high = lax.rem(c - j + 9, 8), lax.rem(c + j - 1, 8)
        for way, block, to, cond in (
            (0, low, up, (c < 7) & (c >= j - 1)),
            (1, high, dn, (c > 0) & (c + j <= 8)),
        ):
            chain[j, key, way] = start(ref(block), ref(block), (s, to), cond)

    def arrive(j, key):
        pl.when(c >= j)(lambda: chain[j, key, 0].wait_recv())
        pl.when(c + j <= 7)(lambda: chain[j, key, 1].wait_recv())

    def tok_send(j, h):
        pass_along(j, h, lambda block: xbuf.at[block, pl.ds(2 * h, 2)])

    def last_send(j):
        pass_along(j, "last", lambda block: last.at[block])

    def tok_step(j, h):
        arrive(j, h)
        if j < 7:
            tok_send(j + 1, h)

    def last_step(j):
        arrive(j, "last")
        if j < 7:
            last_send(j + 1)

    def one(which, d, zz, rows):
        px, py = (xs(d), y) if which == "x" else (x, ys(d))
        return wbuf.at[px, py, zz, k, rows]

    def line(which, d, zz, rows):
        if which == "x":
            return wbuf.at[xs(d), pl.ds(0, 4), zz, k, rows]
        return wbuf.at[pl.ds(0, 4), ys(d), zz, k, rows]

    def to(which, d):
        return at(px=xs(d)) if which == "x" else at(py=ys(d))

    ORDER = (("x", "y", 0), ("y", "x", 32))

    class Gather:
        def __init__(self, zz, own):
            self.zz, self.own = zz, own
            self.sib, self.near, self.far, self.turned, self.passed = [], {}, [], {}, []
            for first, _, r in ORDER:
                rows = pl.ds(r, 32)
                src = w.at[rows] if own else one(first, 0, zz, rows)
                for d in (1, -1):
                    self.near[first, d] = start(src, one(first, 0, zz, rows), to(first, d))
            for first, second, r in ORDER:
                self.turn(first, second, r, 0)

        def turn(self, first, second, r, p):
            ref = one(first, p, self.zz, pl.ds(r, 32))
            src = w.at[pl.ds(r, 32)] if self.own and p == 0 else ref
            for d in (1, -1):
                self.turned[second, p, d] = start(src, ref, to(second, d))

        def half(self, r, d):
            return pl.ds(r + (0 if d == 1 else 16), 16)

        def pass_turned(self, first, second, r, p):
            for d in (1, -1):
                self.turned[second, p, d].wait_recv()
                px, py = (xs(p), ys(-d)) if second == "y" else (xs(-d), ys(p))
                ref = wbuf.at[px, py, self.zz, k, self.half(r, d)]
                self.passed.append(start(ref, ref, to(second, d)))

        def to_sibling(self, second, d, r):
            ref = line(second, d, self.zz, pl.ds(r, 32))
            self.sib.append(start(ref, ref, sibling))

        def step1(self):
            for first, second, r in ORDER:
                for d in (1, -1):
                    self.near[first, d].wait_recv()
                    ref = one(first, -d, self.zz, self.half(r, d))
                    self.far.append(start(ref, ref, to(first, d)))
                    self.turn(first, second, r, -d)
            for first, second, r in ORDER:
                self.pass_turned(first, second, r, 0)

        def step2(self):
            for copy in self.far:
                copy.wait_recv()
            for first, second, r in ORDER:
                self.turn(first, second, r, 2)
            for first, second, r in ORDER:
                self.to_sibling(second, 0, r)
            for p in (1, -1):
                for first, second, r in ORDER:
                    self.pass_turned(first, second, r, p)

        def step3(self):
            for first, second, r in ORDER:
                self.pass_turned(first, second, r, 2)
            for _, second, r in ORDER:
                for d in (1, -1):
                    self.to_sibling(second, d, r)

        def step4(self):
            for copy in self.passed:
                copy.wait_recv()
            for _, second, r in ORDER:
                self.to_sibling(second, 2, r)

        def wait_sibling(self):
            for copy in self.sib:
                copy.wait_recv()

    def leg(way, r):
        return start(w.at[pl.ds(32 * way + r, 16)], legs.at[way, pl.ds(r, 16)], z_dn if way else z_up)

    def next_leg(way, r):
        zz = lax.rem(zh + over, 2)
        dst = wbuf.at[x, y, zz if way else 1 - zz, k, pl.ds(32 * way + r, 16)]
        return start(legs.at[way, pl.ds(r, 16)], dst, z_dn if way else z_up)

    leg1 = [leg(way, r) for r in (0, 16) for way in (0, 1)]
    mine = Gather(zh, True)
    keep_w = pltpu.make_async_copy(w, wbuf.at[x, y, zh, k], loc.at[0])
    keep_w.start()
    packed[...] = jnp.zeros_like(packed)
    for j in range(4):
        xbuf[c, j] = tok[:, j * 128 : (j + 1) * 128]
        packed[2 * j : 2 * j + 2, :] = tok[ROWS - 16 :, j * 128 : (j + 1) * 128].astype(F32)[14:, :]
    last_out[...] = packed[...].astype(BF16)
    handed = start(last_out, last_in, after)

    def tables():
        acc[...] = jnp.zeros_like(acc)
        rate = poles[...] * (-1.0 / SEQ)
        decay[...] = jnp.exp(rate)
        powers[0] = jnp.exp(rate * ROWS)
        powers[1] = jnp.exp(rate * (2.0 * ROWS))
        powers[2] = jnp.exp(rate * (4.0 * ROWS))
        sub = lax.broadcasted_iota(jnp.int32, (SUBS, CH), 0).astype(F32)
        for n in range(MODES):
            r = poles[n : n + 1, :] * (-STEPS / SEQ)
            head_w[n] = jnp.exp(r * sub)
            tail_w[n] = jnp.exp(r * (SUBS - 1.0 - sub))

    def add_dot(cc, left, right):
        for g in range(3):
            dot = jnp.dot(left, right(pl.ds(g * CH, CH)), preferred_element_type=F32)
            for lg in range(4):
                acc[4 * g + lg] += dot[:, lg * 128 : (lg + 1) * 128]

    row = lax.broadcasted_iota(jnp.int32, (TOP, 128), 0)

    def features(cc, j):
        top = jnp.where((row >= 2 * j) & (row < 2 * j + 2), last[cc].astype(F32), 0.0).astype(BF16)
        return jnp.concatenate([top, xbuf[cc, j]], axis=0)

    def dot_z(zz, cc):
        px, py = lax.div(cc, 2), lax.rem(cc, 2) * 2
        left = jnp.concatenate([features(cc, zz), features(cc, zz + 2)], axis=1)
        add_dot(cc, left, lambda cols: wbuf[px, pl.ds(py, 2), zz, :, :, cols].reshape(256, CH))

    def dot_y(p, cc):
        px, py = lax.div(cc, 2), lax.rem(cc, 2) * 2 + p
        left = jnp.concatenate([features(cc, 2 * p), features(cc, 2 * p + 1)], axis=1)
        add_dot(cc, left, lambda cols: wbuf[px, py, :, :, :, cols].reshape(256, CH))

    def dots(kind, which, lo, hi):
        def body(j, _):
            pl.when(c >= j)(lambda: kind(which, lax.rem(c - j + 8, 8)))
            pl.when((j > 0) & (c + j <= 7))(lambda: kind(which, lax.rem(c + j, 8)))
            return 0

        lax.fori_loop(lo, hi, body, 0)

    mine.step1()
    leg2 = []
    for copy, (r, way) in zip(leg1, ((0, 0), (0, 1), (16, 0), (16, 1))):
        copy.wait_recv()
        leg2.append(next_leg(way, r))
    tok_send(1, 0)
    tok_send(1, 1)
    keep_w.wait()
    mine.step2()
    tables()
    mine.step3()
    handed.wait_recv()
    last[c] = jnp.where(s > 0, last_in[...].astype(F32), 0.0).astype(BF16)
    last_send(1)
    tok_step(1, 0)
    for copy in leg2:
        copy.wait_recv()
    theirs = Gather(1 - zh, False)
    mine.step4()
    tok_step(1, 1)
    last_step(1)
    theirs.step1()
    tok_step(2, 0)
    last_step(2)
    tok_step(2, 1)
    theirs.step2()
    tok_step(3, 0)
    mine.wait_sibling()
    dots(dot_z, zh, 0, 2)
    tok_step(3, 1)
    last_step(3)
    theirs.step3()
    tok_step(4, 0)
    dots(dot_z, zh, 2, 4)
    tok_step(4, 1)
    theirs.step4()
    last_step(4)
    tok_step(5, 0)
    tok_step(5, 1)
    last_step(5)
    dots(dot_z, zh, 4, 6)
    theirs.wait_sibling()
    dots(dot_z, 1 - zh, 0, 6)
    tok_step(6, 0)
    tok_step(6, 1)
    last_step(6)
    dots(dot_z, zh, 6, 7)
    dots(dot_z, 1 - zh, 6, 7)
    tok_step(7, 0)
    last_step(7)
    dots(dot_y, 0, 7, 8)
    tok_step(7, 1)
    dots(dot_y, 1, 7, 8)
    for i in range(12):
        for r in range(2):
            two = [acc[i, 2 * j + r : 2 * j + r + 1, :] for j in range(4)]
            acc[i, TOP - 2 + r : TOP - 1 + r, :] = total(two)

    def lanes(lg):
        return pl.ds(pl.multiple_of(lg * 128, 128), 128)

    def rows_of(ref, lg):
        return [jnp.broadcast_to(ref[n : n + 1, lanes(lg)], (SUBS, 128)) for n in range(MODES)]

    def filter_of(g, lg):
        t = [jnp.broadcast_to(taps[i, g : g + 1, lanes(lg)], (SUBS, 128)) for i in range(3)]

        def load(first):
            return rounded(acc[4 * g + lg, pl.ds(first, SUBS, stride=STEPS), :])

        return lambda p0, p1, p2: t[0] * p0 + t[1] * p1 + t[2] * p2, load

    def gate(fk, fv, k3, v3):
        return rounded(fk(*k3) * fv(*v3))

    def pass_a(lg):
        (fk, lk), (fv, lv) = filter_of(1, lg), filter_of(2, lg)
        a = rows_of(decay, lg)

        def body(i, held):
            k1, k2, v1, v2, st = held
            k0, v0 = lk(TOP + i), lv(TOP + i)
            g = gate(fk, fv, (k0, k1, k2), (v0, v1, v2))
            gbuf[i, :, lanes(lg)] = g
            return k0, k1, v0, v1, tuple(a[n] * st[n] + g for n in range(MODES))

        zero = tuple(jnp.zeros((SUBS, 128), F32) for _ in range(MODES))
        held = lax.fori_loop(0, STEPS, body, (lk(TOP - 1), lk(TOP - 2), lv(TOP - 1), lv(TOP - 2), zero), unroll=4)
        for n in range(MODES):
            ends[n, :, lanes(lg)] = held[4][n]
            state[n : n + 1, lanes(lg)] = jnp.sum(tail_w[n, :, lanes(lg)] * held[4][n], axis=0, keepdims=True)

    half = pl.ds(pl.multiple_of(k * 256, 256), 256)
    other = pl.ds(pl.multiple_of((1 - k) * 256, 256), 256)
    own_groups, other_groups = (2 * k, 2 * k + 1), (2 - 2 * k, 3 - 2 * k)
    for lg in other_groups:
        pass_a(lg)
    first = start(state.at[:, other], sib_state.at[:, other], sibling)
    for lg in own_groups:
        pass_a(lg)
    second = start(state.at[:, half], sib_state.at[:, half], sibling)

    def pass_b(lg):
        fq, lq = filter_of(0, lg)
        a, r = rows_of(decay, lg), rows_of(res, lg)
        gain = jnp.broadcast_to(skip[0:1, lanes(lg)], (SUBS, 128))

        def body(i, held):
            q1, q2, st = held
            q0 = lq(TOP + i)
            qbuf[i, :, lanes(lg)] = fq(q0, q1, q2)
            g = gbuf[i, :, lanes(lg)]
            st = tuple(a[n] * st[n] + g for n in range(MODES))
            ybuf[i, :, lanes(lg)] = total([r[n] * st[n] for n in range(MODES)] + [gain * g])
            return q0, q1, st

        zero = tuple(jnp.zeros((SUBS, 128), F32) for _ in range(MODES))
        lax.fori_loop(0, STEPS, body, (lq(TOP - 1), lq(TOP - 2), zero), unroll=2)
        sub = lax.broadcasted_iota(jnp.int32, (SUBS, 128), 0)

        def down(value, by):
            return jnp.where(sub >= by, pltpu.roll(value, by, 0), 0.0)

        for n in range(MODES):
            v = down(ends[n, :, lanes(lg)], 1)
            for by in (1, 2, 4):
                v = v + head_w[n, by : by + 1, lanes(lg)] * down(v, by)
            prefix[n, :, lanes(lg)] = v

    first.wait_recv()
    own, sib = state[:, half], sib_state[:, half]
    chip = powers[0, :, half] * jnp.where(k == 0, own, sib) + jnp.where(k == 0, sib, own)
    c_msg[...] = chip
    q = 4 * x + y
    level = []
    for dx, dy in steps:
        later = 4 * xs(dx) + ys(dy) > q
        level.append(start(c_msg, y_in.at[q], at(px=xs(dx), py=ys(dy)), later))
    pass_b(0)
    pass_b(1)
    drain()
    for (dx, dy), copy in zip(steps, level):
        pl.when(4 * xs(-dx) + ys(-dy) < q)(lambda copy=copy: copy.wait_recv())
    d4 = powers[2, :, half]
    plane = lax.fori_loop(0, q, lambda i, got: got * d4 + y_in[i], jnp.zeros_like(chip))
    z_msg[...] = jnp.where(zh == 0, d4 * plane + chip, plane)
    level = start(z_msg, z_in, opposite)
    second.wait_recv()
    pass_b(2)
    pass_b(3)
    level.wait_recv()
    into = powers[1, :, half] * plane + z_in[...]
    k_msg[...] = into
    level = start(k_msg, k_in, sibling)

    def keep(where, value):
        carry[:, where] = jnp.where(k == 0, value, powers[0, :, where] * value + sib_state[:, where])

    keep(half, into)

    def pass_c(lg):
        a, r = rows_of(decay, lg), rows_of(res, lg)
        ws = tuple(
            r[n] * (prefix[n, :, lanes(lg)] + head_w[n, :, lanes(lg)] * carry[n : n + 1, lanes(lg)])
            for n in range(MODES)
        )

        def body(i, ws):
            ws = tuple(a[n] * ws[n] for n in range(MODES))
            value = ybuf[i, :, lanes(lg)] + total(list(ws))
            obuf[lg, pl.ds(i, SUBS, stride=STEPS), :] = qbuf[i, :, lanes(lg)] * value
            return ws

        lax.fori_loop(0, STEPS, body, ws, unroll=4)
        out[:, lanes(lg)] = obuf[lg].astype(BF16)

    for lg in own_groups:
        pass_c(lg)
    level.wait_recv()
    keep(other, k_in[...])
    for lg in other_groups:
        pass_c(lg)

    drain()


def total(values):
    while len(values) > 1:
        values = [a + b for a, b in zip(values[::2], values[1::2])] + values[len(values) & ~1 :]
    return values[0]


def local(tokens, w_in, short_taps, residues, poles, skip_gain):
    vmem = pl.BlockSpec(memory_space=pltpu.VMEM)
    block = pltpu.VMEM((STEPS, SUBS, CH), F32)
    table = pltpu.VMEM((MODES, SUBS, CH), F32)
    full, part = pltpu.VMEM((MODES, CH), F32), pltpu.VMEM((MODES, CH // 2), F32)
    last = pltpu.VMEM((16, 128), BF16)
    return pl.pallas_call(
        kernel,
        out_shape=jax.ShapeDtypeStruct((ROWS, CH), BF16),
        in_specs=[vmem] * 6,
        out_specs=vmem,
        scratch_shapes=[
            pltpu.VMEM((4, 4, 2, 2, DEPTH, 3 * CH), BF16),
            pltpu.VMEM((8, 4, ROWS, 128), BF16),
            pltpu.VMEM((12, TOP + ROWS, 128), F32),
            pltpu.VMEM((2, DEPTH // 2, 3 * CH), BF16),
            block, block, block,
            pltpu.VMEM((4, ROWS, 128), F32),
            table, table, full, table, table,
            pltpu.VMEM((3, MODES, CH), F32),
            full, full, part, pltpu.VMEM((16, MODES, CH // 2), F32), part, part, part, part, full,
            pltpu.VMEM((16, 128), F32), last, last, pltpu.VMEM((8, 16, 128), BF16),
            pltpu.SemaphoreType.DMA((COPIES,)),
            pltpu.SemaphoreType.DMA((COPIES,)),
            pltpu.SemaphoreType.DMA((1,)),
        ],
        compiler_params=pltpu.CompilerParams(
            collective_id=0, has_side_effects=True, vmem_limit_bytes=40 * 1024 * 1024
        ),
    )(tokens, w_in.reshape(DEPTH, 3 * CH), short_taps, residues, poles, skip_gain.reshape(1, CH))


def solution(mesh):
    placed = (
        P("seq", "chan"),
        P("seq", None, "chan"),
        P(None, None, "chan"),
        P(None, "chan"),
        P(None, "chan"),
        P("chan"),
    )
    return jax.shard_map(
        local, mesh=mesh, in_specs=placed, out_specs=P("seq", "chan"), check_vma=False
    )
```

```python
import jax
import jax.numpy as jnp
from jax import lax
from jax.experimental import pallas as pl
from jax.experimental.pallas import tpu as pltpu
from jax.sharding import PartitionSpec as P

MESH = pl.DeviceIdType.MESH
F32, BF16 = jnp.float32, jnp.bfloat16
ROWS = 256
CH = 512
DEPTH = 64
MODES = 16
SEQ = 16384.0
SUBS = 8
STEPS = ROWS // SUBS
TOP = 16
SENDS, RECVS = 68, 81


def rounded(value):
    return value.astype(BF16).astype(F32)


def kernel(
    tok, w, taps, res, poles, skip, out,
    wbuf, xbuf, acc, legs, gbuf, ybuf, qbuf, obuf, ends, prefix, decay, tail_w, head_w, powers,
    state, sib_state, c_msg, y_in, z_msg, z_in, k_msg, k_in, carry, packed, last_out, last_in, last,
    send, recv, loc,
):
    s, c = lax.axis_index("seq"), lax.axis_index("chan")
    k, zh = lax.rem(s, 2), lax.rem(lax.div(s, 2), 2)
    y, x = lax.rem(lax.div(s, 4), 4), lax.div(s, 16)

    def at(px=x, py=y, pzh=zh, pk=k, pc=c):
        return (((px * 4 + py) * 2 + pzh) * 2 + pk, pc)

    def xs(d):
        return lax.rem(x + d + 4, 4)

    def ys(d):
        return lax.rem(y + d + 4, 4)

    over = lax.div(c + 4, 8)
    far_c = lax.rem(c + 4, 8)
    z_up = at(pzh=lax.rem(zh + over, 2), pc=far_c)
    z_dn = at(pzh=lax.rem(zh + over + 1, 2), pc=far_c)
    sibling = at(pk=1 - k)
    opposite = at(pzh=1 - zh)
    up, dn = lax.rem(c + 1, 8), lax.rem(c + 7, 8)
    after, before = (lax.rem(s + 1, 64), c), (lax.rem(s + 63, 64), c)

    barrier = pltpu.get_barrier_semaphore()
    partners = [sibling, opposite, z_up, z_dn, (s, up), (s, dn), after, before]
    steps = [(dx, dy) for dx in range(4) for dy in range(4) if dx or dy]
    partners += [at(px=xs(dx), py=ys(dy)) for dx, dy in steps]
    for partner in partners:
        pl.semaphore_signal(barrier, inc=1, device_id=partner, device_id_type=MESH)
    pl.semaphore_wait(barrier, len(partners))

    sent, done, send_ids, recv_ids = [], [], {}, {}

    def start(src, dst, to, cond=None, out_group=None, in_group=None):
        out_id = send_ids.setdefault(out_group or ("one", len(send_ids)), len(send_ids))
        in_id = recv_ids.setdefault(in_group or ("one", len(recv_ids)), len(recv_ids))
        copy = pltpu.make_async_remote_copy(
            src_ref=src, dst_ref=dst, send_sem=send.at[out_id], recv_sem=recv.at[in_id],
            device_id=to, device_id_type=MESH,
        )
        if cond is None:
            copy.start()
        else:
            pl.when(cond)(lambda: copy.start())
        if out_group is None:
            sent.append((copy, cond))
        return copy

    def of_group(blocks, out_group=None, in_group=None):
        ref = {
            1: wbuf.at[0, 0, 0, 0], 2: wbuf.at[0, 0, 0], 4: wbuf.at[0, 0],
            8: wbuf.at[0, pl.ds(0, 4), 0], 16: wbuf.at[0], 32: wbuf.at[pl.ds(0, 2)],
        }[blocks]
        return pltpu.make_async_remote_copy(
            src_ref=ref, dst_ref=ref, send_sem=send.at[send_ids.get(out_group, 0)],
            recv_sem=recv.at[recv_ids.get(in_group, 0)], device_id=sibling, device_id_type=MESH,
        )

    def drain():
        for copy, cond in sent[len(done) :]:
            if cond is None:
                copy.wait_send()
            else:
                pl.when(cond)(lambda copy=copy: copy.wait_send())
            done.append(copy)

    def drain_groups():
        for group, blocks in (("leg", 2), ("near", 4), ("far", 2), ("turned", 16), ("passed", 8), ("sib", 32)):
            of_group(blocks, out_group=group).wait_send()

    chain = {}

    def pass_along(j, key, ref):
        low, high = lax.rem(c - j + 9, 8), lax.rem(c + j - 1, 8)
        for way, block, to, cond in (
            (0, low, up, (c < 7) & (c >= j - 1)),
            (1, high, dn, (c > 0) & (c + j <= 8)),
        ):
            chain[j, key, way] = start(ref(block), ref(block), (s, to), cond)

    def arrive(j, key):
        pl.when(c >= j)(lambda: chain[j, key, 0].wait_recv())
        pl.when(c + j <= 7)(lambda: chain[j, key, 1].wait_recv())

    def tok_send(j, h):
        pass_along(j, h, lambda block: xbuf.at[block, pl.ds(2 * h, 2)])

    def last_send(j):
        pass_along(j, "last", lambda block: last.at[block])

    def tok_step(j, h):
        arrive(j, h)
        if j < 7:
            tok_send(j + 1, h)

    def last_step(j):
        arrive(j, "last")
        if j < 7:
            last_send(j + 1)

    def one(which, d, zz, rows):
        px, py = (xs(d), y) if which == "x" else (x, ys(d))
        return wbuf.at[px, py, zz, k, rows]

    def line(which, d, zz, rows):
        if which == "x":
            return wbuf.at[xs(d), pl.ds(0, 4), zz, k, rows]
        return wbuf.at[pl.ds(0, 4), ys(d), zz, k, rows]

    def to(which, d):
        return at(px=xs(d)) if which == "x" else at(py=ys(d))

    ORDER = (("x", "y", 0), ("y", "x", 32))

    class Gather:
        def __init__(self, zz, name):
            self.zz, self.name = zz, name
            for first, _, r in ORDER:
                rows = pl.ds(r, 32)
                src = w.at[rows] if name == "mine" else one(first, 0, zz, rows)
                for d in (1, -1):
                    self.put(src, one(first, 0, zz, rows), to(first, d), "near")
            for first, second, r in ORDER:
                self.turn(first, second, r, 0, "turned0")

        def put(self, src, dst, where, group, in_group=None):
            start(src, dst, where, out_group=group, in_group=(self.name, in_group or group))

        def got(self, group, blocks):
            of_group(blocks, in_group=(self.name, group)).wait_recv()

        def turn(self, first, second, r, p, group):
            ref = one(first, p, self.zz, pl.ds(r, 32))
            src = w.at[pl.ds(r, 32)] if self.name == "mine" and p == 0 else ref
            for d in (1, -1):
                self.put(src, ref, to(second, d), "turned", group)

        def half(self, r, d):
            return pl.ds(r + (0 if d == 1 else 16), 16)

        def pass_turned(self, p):
            for first, second, r in ORDER:
                for d in (1, -1):
                    px, py = (xs(p), ys(-d)) if second == "y" else (xs(-d), ys(p))
                    ref = wbuf.at[px, py, self.zz, k, self.half(r, d)]
                    self.put(ref, ref, to(second, d), "passed")

        def to_sibling(self, d):
            for _, second, r in ORDER:
                ref = line(second, d, self.zz, pl.ds(r, 32))
                self.put(ref, ref, sibling, "sib")

        def step1(self):
            self.got("near", 2)
            for first, second, r in ORDER:
                for d in (1, -1):
                    ref = one(first, -d, self.zz, self.half(r, d))
                    self.put(ref, ref, to(first, d), "far")
                    self.turn(first, second, r, -d, "turned1")
            self.got("turned0", 2)
            self.pass_turned(0)

        def step2(self):
            self.got("far", 1)
            for first, second, r in ORDER:
                self.turn(first, second, r, 2, "turned2")
            self.to_sibling(0)
            self.got("turned1", 4)
            self.pass_turned(1)
            self.pass_turned(-1)

        def step3(self):
            self.got("turned2", 2)
            self.pass_turned(2)
            self.to_sibling(1)
            self.to_sibling(-1)

        def step4(self):
            self.got("passed", 4)
            self.to_sibling(2)

        def wait_sibling(self):
            self.got("sib", 16)

    def leg(way, r):
        return start(w.at[pl.ds(32 * way + r, 16)], legs.at[way, pl.ds(r, 16)], z_dn if way else z_up, None, "leg")

    def next_leg(way, r):
        zz = lax.rem(zh + over, 2)
        dst = wbuf.at[x, y, zz if way else 1 - zz, k, pl.ds(32 * way + r, 16)]
        return start(legs.at[way, pl.ds(r, 16)], dst, z_dn if way else z_up, None, "leg", "leg2")

    leg1 = [leg(way, r) for r in (0, 16) for way in (0, 1)]
    mine = Gather(zh, "mine")
    keep_w = pltpu.make_async_copy(w, wbuf.at[x, y, zh, k], loc.at[0])
    keep_w.start()
    packed[...] = jnp.zeros_like(packed)
    for j in range(4):
        xbuf[c, j] = tok[:, j * 128 : (j + 1) * 128]
        packed[2 * j : 2 * j + 2, :] = tok[ROWS - 16 :, j * 128 : (j + 1) * 128].astype(F32)[14:, :]
    last_out[...] = packed[...].astype(BF16)
    handed = start(last_out, last_in, after)

    def tables():
        acc[...] = jnp.zeros_like(acc)
        rate = poles[...] * (-1.0 / SEQ)
        decay[...] = jnp.exp(rate)
        powers[0] = jnp.exp(rate * ROWS)
        powers[1] = jnp.exp(rate * (2.0 * ROWS))
        powers[2] = jnp.exp(rate * (4.0 * ROWS))
        sub = lax.broadcasted_iota(jnp.int32, (SUBS, CH), 0).astype(F32)
        for n in range(MODES):
            r = poles[n : n + 1, :] * (-STEPS / SEQ)
            head_w[n] = jnp.exp(r * sub)
            tail_w[n] = jnp.exp(r * (SUBS - 1.0 - sub))

    def add_dot(cc, left, right):
        for g in range(3):
            dot = jnp.dot(left, right(pl.ds(g * CH, CH)), preferred_element_type=F32)
            for lg in range(4):
                acc[4 * g + lg] += dot[:, lg * 128 : (lg + 1) * 128]

    row = lax.broadcasted_iota(jnp.int32, (TOP, 128), 0)

    def features(cc, j):
        top = jnp.where((row >= 2 * j) & (row < 2 * j + 2), last[cc].astype(F32), 0.0).astype(BF16)
        return jnp.concatenate([top, xbuf[cc, j]], axis=0)

    def dot_z(zz, cc):
        px, py = lax.div(cc, 2), lax.rem(cc, 2) * 2
        left = jnp.concatenate([features(cc, zz), features(cc, zz + 2)], axis=1)
        add_dot(cc, left, lambda cols: wbuf[px, pl.ds(py, 2), zz, :, :, cols].reshape(256, CH))

    def dot_y(p, cc):
        px, py = lax.div(cc, 2), lax.rem(cc, 2) * 2 + p
        left = jnp.concatenate([features(cc, 2 * p), features(cc, 2 * p + 1)], axis=1)
        add_dot(cc, left, lambda cols: wbuf[px, py, :, :, :, cols].reshape(256, CH))

    def dots(kind, which, lo, hi):
        def body(j, _):
            pl.when(c >= j)(lambda: kind(which, lax.rem(c - j + 8, 8)))
            pl.when((j > 0) & (c + j <= 7))(lambda: kind(which, lax.rem(c + j, 8)))
            return 0

        lax.fori_loop(lo, hi, body, 0)

    mine.step1()
    for copy, (r, way) in zip(leg1, ((0, 0), (0, 1), (16, 0), (16, 1))):
        copy.wait_recv()
        next_leg(way, r)
    tok_send(1, 0)
    tok_send(1, 1)
    keep_w.wait()
    mine.step2()
    tables()
    mine.step3()
    handed.wait_recv()
    last[c] = jnp.where(s > 0, last_in[...].astype(F32), 0.0).astype(BF16)
    last_send(1)
    tok_step(1, 0)
    of_group(1, in_group="leg2").wait_recv()
    theirs = Gather(1 - zh, "theirs")
    mine.step4()
    tok_step(1, 1)
    last_step(1)
    theirs.step1()
    tok_step(2, 0)
    last_step(2)
    tok_step(2, 1)
    theirs.step2()
    tok_step(3, 0)
    mine.wait_sibling()
    dots(dot_z, zh, 0, 2)
    tok_step(3, 1)
    last_step(3)
    theirs.step3()
    tok_step(4, 0)
    dots(dot_z, zh, 2, 4)
    tok_step(4, 1)
    theirs.step4()
    last_step(4)
    tok_step(5, 0)
    tok_step(5, 1)
    last_step(5)
    dots(dot_z, zh, 4, 6)
    theirs.wait_sibling()
    dots(dot_z, 1 - zh, 0, 6)
    tok_step(6, 0)
    tok_step(6, 1)
    last_step(6)
    dots(dot_z, zh, 6, 7)
    dots(dot_z, 1 - zh, 6, 7)
    tok_step(7, 0)
    last_step(7)
    dots(dot_y, 0, 7, 8)
    tok_step(7, 1)
    dots(dot_y, 1, 7, 8)
    for i in range(12):
        for r in range(2):
            two = [acc[i, 2 * j + r : 2 * j + r + 1, :] for j in range(4)]
            acc[i, TOP - 2 + r : TOP - 1 + r, :] = total(two)

    def lanes(lg):
        return pl.ds(pl.multiple_of(lg * 128, 128), 128)

    def rows_of(ref, lg):
        return [jnp.broadcast_to(ref[n : n + 1, lanes(lg)], (SUBS, 128)) for n in range(MODES)]

    def filter_of(g, lg):
        t = [jnp.broadcast_to(taps[i, g : g + 1, lanes(lg)], (SUBS, 128)) for i in range(3)]

        def load(first):
            return rounded(acc[4 * g + lg, pl.ds(first, SUBS, stride=STEPS), :])

        return lambda p0, p1, p2: t[0] * p0 + t[1] * p1 + t[2] * p2, load

    def gate(fk, fv, k3, v3):
        return rounded(fk(*k3) * fv(*v3))

    def pass_a(lg):
        (fk, lk), (fv, lv) = filter_of(1, lg), filter_of(2, lg)
        a = rows_of(decay, lg)

        def body(i, held):
            k1, k2, v1, v2, st = held
            k0, v0 = lk(TOP + i), lv(TOP + i)
            g = gate(fk, fv, (k0, k1, k2), (v0, v1, v2))
            gbuf[i, :, lanes(lg)] = g
            return k0, k1, v0, v1, tuple(a[n] * st[n] + g for n in range(MODES))

        zero = tuple(jnp.zeros((SUBS, 128), F32) for _ in range(MODES))
        held = lax.fori_loop(0, STEPS, body, (lk(TOP - 1), lk(TOP - 2), lv(TOP - 1), lv(TOP - 2), zero), unroll=4)
        for n in range(MODES):
            ends[n, :, lanes(lg)] = held[4][n]
            state[n : n + 1, lanes(lg)] = jnp.sum(tail_w[n, :, lanes(lg)] * held[4][n], axis=0, keepdims=True)

    half = pl.ds(pl.multiple_of(k * 256, 256), 256)
    other = pl.ds(pl.multiple_of((1 - k) * 256, 256), 256)
    own_groups, other_groups = (2 * k, 2 * k + 1), (2 - 2 * k, 3 - 2 * k)
    for lg in other_groups:
        pass_a(lg)
    first = start(state.at[:, other], sib_state.at[:, other], sibling)
    for lg in own_groups:
        pass_a(lg)
    second = start(state.at[:, half], sib_state.at[:, half], sibling)

    def pass_b(lg):
        fq, lq = filter_of(0, lg)
        a, r = rows_of(decay, lg), rows_of(res, lg)
        gain = jnp.broadcast_to(skip[0:1, lanes(lg)], (SUBS, 128))

        def body(i, held):
            q1, q2, st = held
            q0 = lq(TOP + i)
            qbuf[i, :, lanes(lg)] = fq(q0, q1, q2)
            g = gbuf[i, :, lanes(lg)]
            st = tuple(a[n] * st[n] + g for n in range(MODES))
            ybuf[i, :, lanes(lg)] = total([r[n] * st[n] for n in range(MODES)] + [gain * g])
            return q0, q1, st

        zero = tuple(jnp.zeros((SUBS, 128), F32) for _ in range(MODES))
        lax.fori_loop(0, STEPS, body, (lq(TOP - 1), lq(TOP - 2), zero), unroll=2)
        sub = lax.broadcasted_iota(jnp.int32, (SUBS, 128), 0)

        def down(value, by):
            return jnp.where(sub >= by, pltpu.roll(value, by, 0), 0.0)

        for n in range(MODES):
            v = down(ends[n, :, lanes(lg)], 1)
            for by in (1, 2, 4):
                v = v + head_w[n, by : by + 1, lanes(lg)] * down(v, by)
            prefix[n, :, lanes(lg)] = v

    first.wait_recv()
    own, sib = state[:, half], sib_state[:, half]
    chip = powers[0, :, half] * jnp.where(k == 0, own, sib) + jnp.where(k == 0, sib, own)
    c_msg[...] = chip
    q = 4 * x + y
    level = []
    for dx, dy in steps:
        later = 4 * xs(dx) + ys(dy) > q
        level.append(start(c_msg, y_in.at[q], at(px=xs(dx), py=ys(dy)), later))
    pass_b(0)
    pass_b(1)
    drain()
    drain_groups()
    for (dx, dy), copy in zip(steps, level):
        pl.when(4 * xs(-dx) + ys(-dy) < q)(lambda copy=copy: copy.wait_recv())
    d4 = powers[2, :, half]
    plane = lax.fori_loop(0, q, lambda i, got: got * d4 + y_in[i], jnp.zeros_like(chip))
    z_msg[...] = jnp.where(zh == 0, d4 * plane + chip, plane)
    level = start(z_msg, z_in, opposite)
    second.wait_recv()
    pass_b(2)
    pass_b(3)
    level.wait_recv()
    into = powers[1, :, half] * plane + z_in[...]
    k_msg[...] = into
    level = start(k_msg, k_in, sibling)

    def keep(where, value):
        carry[:, where] = jnp.where(k == 0, value, powers[0, :, where] * value + sib_state[:, where])

    keep(half, into)

    def pass_c(lg):
        a, r = rows_of(decay, lg), rows_of(res, lg)
        ws = tuple(
            r[n] * (prefix[n, :, lanes(lg)] + head_w[n, :, lanes(lg)] * carry[n : n + 1, lanes(lg)])
            for n in range(MODES)
        )

        def body(i, ws):
            ws = tuple(a[n] * ws[n] for n in range(MODES))
            value = ybuf[i, :, lanes(lg)] + total(list(ws))
            obuf[lg, pl.ds(i, SUBS, stride=STEPS), :] = qbuf[i, :, lanes(lg)] * value
            return ws

        lax.fori_loop(0, STEPS, body, ws, unroll=4)
        out[:, lanes(lg)] = obuf[lg].astype(BF16)

    for lg in own_groups:
        pass_c(lg)
    level.wait_recv()
    keep(other, k_in[...])
    for lg in other_groups:
        pass_c(lg)

    drain()


def total(values):
    while len(values) > 1:
        values = [a + b for a, b in zip(values[::2], values[1::2])] + values[len(values) & ~1 :]
    return values[0]


def local(tokens, w_in, short_taps, residues, poles, skip_gain):
    vmem = pl.BlockSpec(memory_space=pltpu.VMEM)
    block = pltpu.VMEM((STEPS, SUBS, CH), F32)
    table = pltpu.VMEM((MODES, SUBS, CH), F32)
    full, part = pltpu.VMEM((MODES, CH), F32), pltpu.VMEM((MODES, CH // 2), F32)
    last = pltpu.VMEM((16, 128), BF16)
    return pl.pallas_call(
        kernel,
        out_shape=jax.ShapeDtypeStruct((ROWS, CH), BF16),
        in_specs=[vmem] * 6,
        out_specs=vmem,
        scratch_shapes=[
            pltpu.VMEM((4, 4, 2, 2, DEPTH, 3 * CH), BF16),
            pltpu.VMEM((8, 4, ROWS, 128), BF16),
            pltpu.VMEM((12, TOP + ROWS, 128), F32),
            pltpu.VMEM((2, DEPTH // 2, 3 * CH), BF16),
            block, block, block,
            pltpu.VMEM((4, ROWS, 128), F32),
            table, table, full, table, table,
            pltpu.VMEM((3, MODES, CH), F32),
            full, full, part, pltpu.VMEM((16, MODES, CH // 2), F32), part, part, part, part, full,
            pltpu.VMEM((16, 128), F32), last, last, pltpu.VMEM((8, 16, 128), BF16),
            pltpu.SemaphoreType.DMA((SENDS,)),
            pltpu.SemaphoreType.DMA((RECVS,)),
            pltpu.SemaphoreType.DMA((1,)),
        ],
        compiler_params=pltpu.CompilerParams(
            collective_id=0, has_side_effects=True, vmem_limit_bytes=40 * 1024 * 1024
        ),
    )(tokens, w_in.reshape(DEPTH, 3 * CH), short_taps, residues, poles, skip_gain.reshape(1, CH))


def solution(mesh):
    placed = (
        P("seq", "chan"),
        P("seq", None, "chan"),
        P(None, None, "chan"),
        P(None, "chan"),
        P(None, "chan"),
        P("chan"),
    )
    return jax.shard_map(
        local, mesh=mesh, in_specs=placed, out_specs=P("seq", "chan"), check_vma=False
    )
```

```python
import jax
import jax.numpy as jnp
from jax import lax
from jax.experimental import pallas as pl
from jax.experimental.pallas import tpu as pltpu
from jax.sharding import PartitionSpec as P

MESH = pl.DeviceIdType.MESH
F32, BF16 = jnp.float32, jnp.bfloat16
ROWS = 256
CH = 512
DEPTH = 64
MODES = 16
SEQ = 16384.0
SUBS = 8
STEPS = ROWS // SUBS
TOP = 16
SENDS, RECVS = 44, 81


def rounded(value):
    return value.astype(BF16).astype(F32)


def kernel(
    tok, w, taps, res, poles, skip, out,
    wbuf, xbuf, acc, legs, gbuf, ybuf, qbuf, obuf, ends, prefix, decay, tail_w, head_w, powers,
    state, sib_state, c_msg, y_in, z_msg, z_in, k_msg, k_in, carry, packed, last_out, last_in, last,
    send, recv, loc,
):
    s, c = lax.axis_index("seq"), lax.axis_index("chan")
    k, zh = lax.rem(s, 2), lax.rem(lax.div(s, 2), 2)
    y, x = lax.rem(lax.div(s, 4), 4), lax.div(s, 16)

    def at(px=x, py=y, pzh=zh, pk=k, pc=c):
        return (((px * 4 + py) * 2 + pzh) * 2 + pk, pc)

    def xs(d):
        return lax.rem(x + d + 4, 4)

    def ys(d):
        return lax.rem(y + d + 4, 4)

    over = lax.div(c + 4, 8)
    far_c = lax.rem(c + 4, 8)
    z_up = at(pzh=lax.rem(zh + over, 2), pc=far_c)
    z_dn = at(pzh=lax.rem(zh + over + 1, 2), pc=far_c)
    sibling = at(pk=1 - k)
    opposite = at(pzh=1 - zh)
    up, dn = lax.rem(c + 1, 8), lax.rem(c + 7, 8)
    after, before = (lax.rem(s + 1, 64), c), (lax.rem(s + 63, 64), c)

    barrier = pltpu.get_barrier_semaphore()
    partners = [sibling, opposite, z_up, z_dn, (s, up), (s, dn), after, before]
    steps = [(dx, dy) for dx in range(4) for dy in range(4) if dx or dy]
    partners += [at(px=xs(dx), py=ys(dy)) for dx, dy in steps]
    for partner in partners:
        pl.semaphore_signal(barrier, inc=1, device_id=partner, device_id_type=MESH)
    pl.semaphore_wait(barrier, len(partners))

    sent, done, send_ids, recv_ids = [], [], {}, {}

    def start(src, dst, to, cond=None, out_group=None, in_group=None):
        out_id = send_ids.setdefault(out_group or ("one", len(send_ids)), len(send_ids))
        in_id = recv_ids.setdefault(in_group or ("one", len(recv_ids)), len(recv_ids))
        copy = pltpu.make_async_remote_copy(
            src_ref=src, dst_ref=dst, send_sem=send.at[out_id], recv_sem=recv.at[in_id],
            device_id=to, device_id_type=MESH,
        )
        if cond is None:
            copy.start()
        else:
            pl.when(cond)(lambda: copy.start())
        if out_group is None:
            sent.append((copy, cond))
        return copy

    def of_group(blocks, out_group=None, in_group=None):
        ref = {
            1: wbuf.at[0, 0, 0, 0], 2: wbuf.at[0, 0, 0], 4: wbuf.at[0, 0],
            8: wbuf.at[0, pl.ds(0, 4), 0], 16: wbuf.at[0], 32: wbuf.at[pl.ds(0, 2)],
        }[blocks]
        return pltpu.make_async_remote_copy(
            src_ref=ref, dst_ref=ref, send_sem=send.at[send_ids.get(out_group, 0)],
            recv_sem=recv.at[recv_ids.get(in_group, 0)], device_id=sibling, device_id_type=MESH,
        )

    def drain():
        for copy, cond in sent[len(done) :]:
            if cond is None:
                copy.wait_send()
            else:
                pl.when(cond)(lambda copy=copy: copy.wait_send())
            done.append(copy)

    def drain_groups():
        for copy, cond in chained.values():
            pl.when(cond)(lambda copy=copy: copy.wait_send())
        for group, blocks in (("leg", 2), ("near", 4), ("far", 2), ("turned", 16), ("passed", 8), ("sib", 32)):
            of_group(blocks, out_group=group).wait_send()

    chain, chained = {}, {}

    def pass_along(j, key, ref):
        low, high = lax.rem(c - j + 9, 8), lax.rem(c + j - 1, 8)
        for way, block, to, cond in (
            (0, low, up, (c < 7) & (c >= j - 1)),
            (1, high, dn, (c > 0) & (c + j <= 8)),
        ):
            if (j - 3, key, way) in chain:
                before_cond = (c < 7) & (c >= j - 4) if way == 0 else (c > 0) & (c + j <= 11)
                old = chain[j - 3, key, way]
                pl.when(before_cond)(lambda: old.wait_send())
            chain[j, key, way] = start(ref(block), ref(block), (s, to), cond, ("chain", j % 3, key, way))
            chained[j % 3, key, way] = chain[j, key, way], cond

    def arrive(j, key):
        pl.when(c >= j)(lambda: chain[j, key, 0].wait_recv())
        pl.when(c + j <= 7)(lambda: chain[j, key, 1].wait_recv())

    def tok_send(j, h):
        pass_along(j, h, lambda block: xbuf.at[block, pl.ds(2 * h, 2)])

    def last_send(j):
        pass_along(j, "last", lambda block: last.at[block])

    def tok_step(j, h):
        arrive(j, h)
        if j < 7:
            tok_send(j + 1, h)

    def last_step(j):
        arrive(j, "last")
        if j < 7:
            last_send(j + 1)

    def one(which, d, zz, rows):
        px, py = (xs(d), y) if which == "x" else (x, ys(d))
        return wbuf.at[px, py, zz, k, rows]

    def line(which, d, zz, rows):
        if which == "x":
            return wbuf.at[xs(d), pl.ds(0, 4), zz, k, rows]
        return wbuf.at[pl.ds(0, 4), ys(d), zz, k, rows]

    def to(which, d):
        return at(px=xs(d)) if which == "x" else at(py=ys(d))

    ORDER = (("x", "y", 0), ("y", "x", 32))

    class Gather:
        def __init__(self, zz, name):
            self.zz, self.name = zz, name
            for first, _, r in ORDER:
                rows = pl.ds(r, 32)
                src = w.at[rows] if name == "mine" else one(first, 0, zz, rows)
                for d in (1, -1):
                    self.put(src, one(first, 0, zz, rows), to(first, d), "near")
            for first, second, r in ORDER:
                self.turn(first, second, r, 0, "turned0")

        def put(self, src, dst, where, group, in_group=None):
            start(src, dst, where, out_group=group, in_group=(self.name, in_group or group))

        def got(self, group, blocks):
            of_group(blocks, in_group=(self.name, group)).wait_recv()

        def turn(self, first, second, r, p, group):
            ref = one(first, p, self.zz, pl.ds(r, 32))
            src = w.at[pl.ds(r, 32)] if self.name == "mine" and p == 0 else ref
            for d in (1, -1):
                self.put(src, ref, to(second, d), "turned", group)

        def half(self, r, d):
            return pl.ds(r + (0 if d == 1 else 16), 16)

        def pass_turned(self, p):
            for first, second, r in ORDER:
                for d in (1, -1):
                    px, py = (xs(p), ys(-d)) if second == "y" else (xs(-d), ys(p))
                    ref = wbuf.at[px, py, self.zz, k, self.half(r, d)]
                    self.put(ref, ref, to(second, d), "passed")

        def to_sibling(self, d):
            for _, second, r in ORDER:
                ref = line(second, d, self.zz, pl.ds(r, 32))
                self.put(ref, ref, sibling, "sib")

        def step1(self):
            self.got("near", 2)
            for first, second, r in ORDER:
                for d in (1, -1):
                    ref = one(first, -d, self.zz, self.half(r, d))
                    self.put(ref, ref, to(first, d), "far")
                    self.turn(first, second, r, -d, "turned1")
            self.got("turned0", 2)
            self.pass_turned(0)

        def step2(self):
            self.got("far", 1)
            for first, second, r in ORDER:
                self.turn(first, second, r, 2, "turned2")
            self.to_sibling(0)
            self.got("turned1", 4)
            self.pass_turned(1)
            self.pass_turned(-1)

        def step3(self):
            self.got("turned2", 2)
            self.pass_turned(2)
            self.to_sibling(1)
            self.to_sibling(-1)

        def step4(self):
            self.got("passed", 4)
            self.to_sibling(2)

        def wait_sibling(self):
            self.got("sib", 16)

    def leg(way, r):
        return start(w.at[pl.ds(32 * way + r, 16)], legs.at[way, pl.ds(r, 16)], z_dn if way else z_up, None, "leg")

    def next_leg(way, r):
        zz = lax.rem(zh + over, 2)
        dst = wbuf.at[x, y, zz if way else 1 - zz, k, pl.ds(32 * way + r, 16)]
        return start(legs.at[way, pl.ds(r, 16)], dst, z_dn if way else z_up, None, "leg", "leg2")

    leg1 = [leg(way, r) for r in (0, 16) for way in (0, 1)]
    mine = Gather(zh, "mine")
    keep_w = pltpu.make_async_copy(w, wbuf.at[x, y, zh, k], loc.at[0])
    keep_w.start()
    packed[...] = jnp.zeros_like(packed)
    for j in range(4):
        xbuf[c, j] = tok[:, j * 128 : (j + 1) * 128]
        packed[2 * j : 2 * j + 2, :] = tok[ROWS - 16 :, j * 128 : (j + 1) * 128].astype(F32)[14:, :]
    last_out[...] = packed[...].astype(BF16)
    handed = start(last_out, last_in, after)

    def tables():
        acc[...] = jnp.zeros_like(acc)
        rate = poles[...] * (-1.0 / SEQ)
        decay[...] = jnp.exp(rate)
        powers[0] = jnp.exp(rate * ROWS)
        powers[1] = jnp.exp(rate * (2.0 * ROWS))
        powers[2] = jnp.exp(rate * (4.0 * ROWS))
        sub = lax.broadcasted_iota(jnp.int32, (SUBS, CH), 0).astype(F32)
        for n in range(MODES):
            r = poles[n : n + 1, :] * (-STEPS / SEQ)
            head_w[n] = jnp.exp(r * sub)
            tail_w[n] = jnp.exp(r * (SUBS - 1.0 - sub))

    def add_dot(cc, left, right):
        for g in range(3):
            dot = jnp.dot(left, right(pl.ds(g * CH, CH)), preferred_element_type=F32)
            for lg in range(4):
                acc[4 * g + lg] += dot[:, lg * 128 : (lg + 1) * 128]

    row = lax.broadcasted_iota(jnp.int32, (TOP, 128), 0)

    def features(cc, j):
        top = jnp.where((row >= 2 * j) & (row < 2 * j + 2), last[cc].astype(F32), 0.0).astype(BF16)
        return jnp.concatenate([top, xbuf[cc, j]], axis=0)

    def dot_z(zz, cc):
        px, py = lax.div(cc, 2), lax.rem(cc, 2) * 2
        left = jnp.concatenate([features(cc, zz), features(cc, zz + 2)], axis=1)
        add_dot(cc, left, lambda cols: wbuf[px, pl.ds(py, 2), zz, :, :, cols].reshape(256, CH))

    def dot_y(p, cc):
        px, py = lax.div(cc, 2), lax.rem(cc, 2) * 2 + p
        left = jnp.concatenate([features(cc, 2 * p), features(cc, 2 * p + 1)], axis=1)
        add_dot(cc, left, lambda cols: wbuf[px, py, :, :, :, cols].reshape(256, CH))

    def dots(kind, which, lo, hi):
        def body(j, _):
            pl.when(c >= j)(lambda: kind(which, lax.rem(c - j + 8, 8)))
            pl.when((j > 0) & (c + j <= 7))(lambda: kind(which, lax.rem(c + j, 8)))
            return 0

        lax.fori_loop(lo, hi, body, 0)

    mine.step1()
    for copy, (r, way) in zip(leg1, ((0, 0), (0, 1), (16, 0), (16, 1))):
        copy.wait_recv()
        next_leg(way, r)
    tok_send(1, 0)
    tok_send(1, 1)
    keep_w.wait()
    mine.step2()
    tables()
    mine.step3()
    handed.wait_recv()
    last[c] = jnp.where(s > 0, last_in[...].astype(F32), 0.0).astype(BF16)
    last_send(1)
    tok_step(1, 0)
    of_group(1, in_group="leg2").wait_recv()
    theirs = Gather(1 - zh, "theirs")
    mine.step4()
    tok_step(1, 1)
    last_step(1)
    theirs.step1()
    tok_step(2, 0)
    last_step(2)
    tok_step(2, 1)
    theirs.step2()
    tok_step(3, 0)
    mine.wait_sibling()
    dots(dot_z, zh, 0, 2)
    tok_step(3, 1)
    last_step(3)
    theirs.step3()
    tok_step(4, 0)
    dots(dot_z, zh, 2, 4)
    tok_step(4, 1)
    theirs.step4()
    last_step(4)
    tok_step(5, 0)
    tok_step(5, 1)
    last_step(5)
    dots(dot_z, zh, 4, 6)
    tok_step(6, 0)
    tok_step(6, 1)
    last_step(6)
    theirs.wait_sibling()
    dots(dot_z, 1 - zh, 0, 6)
    dots(dot_z, zh, 6, 7)
    dots(dot_z, 1 - zh, 6, 7)
    tok_step(7, 0)
    last_step(7)
    dots(dot_y, 0, 7, 8)
    tok_step(7, 1)
    dots(dot_y, 1, 7, 8)
    for i in range(12):
        for r in range(2):
            two = [acc[i, 2 * j + r : 2 * j + r + 1, :] for j in range(4)]
            acc[i, TOP - 2 + r : TOP - 1 + r, :] = total(two)

    def lanes(lg):
        return pl.ds(pl.multiple_of(lg * 128, 128), 128)

    def rows_of(ref, lg):
        return [jnp.broadcast_to(ref[n : n + 1, lanes(lg)], (SUBS, 128)) for n in range(MODES)]

    def filter_of(g, lg):
        t = [jnp.broadcast_to(taps[i, g : g + 1, lanes(lg)], (SUBS, 128)) for i in range(3)]

        def load(first):
            return rounded(acc[4 * g + lg, pl.ds(first, SUBS, stride=STEPS), :])

        return lambda p0, p1, p2: t[0] * p0 + t[1] * p1 + t[2] * p2, load

    def gate(fk, fv, k3, v3):
        return rounded(fk(*k3) * fv(*v3))

    def pass_a(lg):
        (fk, lk), (fv, lv) = filter_of(1, lg), filter_of(2, lg)
        a = rows_of(decay, lg)

        def body(i, held):
            k1, k2, v1, v2, st = held
            k0, v0 = lk(TOP + i), lv(TOP + i)
            g = gate(fk, fv, (k0, k1, k2), (v0, v1, v2))
            gbuf[i, :, lanes(lg)] = g
            return k0, k1, v0, v1, tuple(a[n] * st[n] + g for n in range(MODES))

        zero = tuple(jnp.zeros((SUBS, 128), F32) for _ in range(MODES))
        held = lax.fori_loop(0, STEPS, body, (lk(TOP - 1), lk(TOP - 2), lv(TOP - 1), lv(TOP - 2), zero), unroll=4)
        for n in range(MODES):
            ends[n, :, lanes(lg)] = held[4][n]
            state[n : n + 1, lanes(lg)] = jnp.sum(tail_w[n, :, lanes(lg)] * held[4][n], axis=0, keepdims=True)

    half = pl.ds(pl.multiple_of(k * 256, 256), 256)
    other = pl.ds(pl.multiple_of((1 - k) * 256, 256), 256)
    own_groups, other_groups = (2 * k, 2 * k + 1), (2 - 2 * k, 3 - 2 * k)
    for lg in other_groups:
        pass_a(lg)
    first = start(state.at[:, other], sib_state.at[:, other], sibling)
    for lg in own_groups:
        pass_a(lg)
    second = start(state.at[:, half], sib_state.at[:, half], sibling)

    def pass_b(lg):
        fq, lq = filter_of(0, lg)
        a, r = rows_of(decay, lg), rows_of(res, lg)
        gain = jnp.broadcast_to(skip[0:1, lanes(lg)], (SUBS, 128))

        def body(i, held):
            q1, q2, st = held
            q0 = lq(TOP + i)
            qbuf[i, :, lanes(lg)] = fq(q0, q1, q2)
            g = gbuf[i, :, lanes(lg)]
            st = tuple(a[n] * st[n] + g for n in range(MODES))
            ybuf[i, :, lanes(lg)] = total([r[n] * st[n] for n in range(MODES)] + [gain * g])
            return q0, q1, st

        zero = tuple(jnp.zeros((SUBS, 128), F32) for _ in range(MODES))
        lax.fori_loop(0, STEPS, body, (lq(TOP - 1), lq(TOP - 2), zero), unroll=2)
        sub = lax.broadcasted_iota(jnp.int32, (SUBS, 128), 0)

        def down(value, by):
            return jnp.where(sub >= by, pltpu.roll(value, by, 0), 0.0)

        for n in range(MODES):
            v = down(ends[n, :, lanes(lg)], 1)
            for by in (1, 2, 4):
                v = v + head_w[n, by : by + 1, lanes(lg)] * down(v, by)
            prefix[n, :, lanes(lg)] = v

    first.wait_recv()
    own, sib = state[:, half], sib_state[:, half]
    chip = powers[0, :, half] * jnp.where(k == 0, own, sib) + jnp.where(k == 0, sib, own)
    c_msg[...] = chip
    q = 4 * x + y
    level = []
    for dx, dy in steps:
        later = 4 * xs(dx) + ys(dy) > q
        level.append(start(c_msg, y_in.at[q], at(px=xs(dx), py=ys(dy)), later))
    pass_b(0)
    pass_b(1)
    drain()
    drain_groups()
    for (dx, dy), copy in zip(steps, level):
        pl.when(4 * xs(-dx) + ys(-dy) < q)(lambda copy=copy: copy.wait_recv())
    d4 = powers[2, :, half]
    plane = lax.fori_loop(0, q, lambda i, got: got * d4 + y_in[i], jnp.zeros_like(chip))
    z_msg[...] = jnp.where(zh == 0, d4 * plane + chip, plane)
    level = start(z_msg, z_in, opposite)
    second.wait_recv()
    pass_b(2)
    pass_b(3)
    level.wait_recv()
    into = powers[1, :, half] * plane + z_in[...]
    k_msg[...] = into
    level = start(k_msg, k_in, sibling)

    def keep(where, value):
        carry[:, where] = jnp.where(k == 0, value, powers[0, :, where] * value + sib_state[:, where])

    keep(half, into)

    def pass_c(lg):
        a, r = rows_of(decay, lg), rows_of(res, lg)
        ws = tuple(
            r[n] * (prefix[n, :, lanes(lg)] + head_w[n, :, lanes(lg)] * carry[n : n + 1, lanes(lg)])
            for n in range(MODES)
        )

        def body(i, ws):
            ws = tuple(a[n] * ws[n] for n in range(MODES))
            value = ybuf[i, :, lanes(lg)] + total(list(ws))
            obuf[lg, pl.ds(i, SUBS, stride=STEPS), :] = qbuf[i, :, lanes(lg)] * value
            return ws

        lax.fori_loop(0, STEPS, body, ws, unroll=4)
        out[:, lanes(lg)] = obuf[lg].astype(BF16)

    for lg in own_groups:
        pass_c(lg)
    level.wait_recv()
    keep(other, k_in[...])
    for lg in other_groups:
        pass_c(lg)

    drain()


def total(values):
    while len(values) > 1:
        values = [a + b for a, b in zip(values[::2], values[1::2])] + values[len(values) & ~1 :]
    return values[0]


def local(tokens, w_in, short_taps, residues, poles, skip_gain):
    vmem = pl.BlockSpec(memory_space=pltpu.VMEM)
    block = pltpu.VMEM((STEPS, SUBS, CH), F32)
    table = pltpu.VMEM((MODES, SUBS, CH), F32)
    full, part = pltpu.VMEM((MODES, CH), F32), pltpu.VMEM((MODES, CH // 2), F32)
    last = pltpu.VMEM((16, 128), BF16)
    return pl.pallas_call(
        kernel,
        out_shape=jax.ShapeDtypeStruct((ROWS, CH), BF16),
        in_specs=[vmem] * 6,
        out_specs=vmem,
        scratch_shapes=[
            pltpu.VMEM((4, 4, 2, 2, DEPTH, 3 * CH), BF16),
            pltpu.VMEM((8, 4, ROWS, 128), BF16),
            pltpu.VMEM((12, TOP + ROWS, 128), F32),
            pltpu.VMEM((2, DEPTH // 2, 3 * CH), BF16),
            block, block, block,
            pltpu.VMEM((4, ROWS, 128), F32),
            table, table, full, table, table,
            pltpu.VMEM((3, MODES, CH), F32),
            full, full, part, pltpu.VMEM((16, MODES, CH // 2), F32), part, part, part, part, full,
            pltpu.VMEM((16, 128), F32), last, last, pltpu.VMEM((8, 16, 128), BF16),
            pltpu.SemaphoreType.DMA((SENDS,)),
            pltpu.SemaphoreType.DMA((RECVS,)),
            pltpu.SemaphoreType.DMA((1,)),
        ],
        compiler_params=pltpu.CompilerParams(
            collective_id=0, has_side_effects=True, vmem_limit_bytes=40 * 1024 * 1024
        ),
    )(tokens, w_in.reshape(DEPTH, 3 * CH), short_taps, residues, poles, skip_gain.reshape(1, CH))


def solution(mesh):
    placed = (
        P("seq", "chan"),
        P("seq", None, "chan"),
        P(None, None, "chan"),
        P(None, "chan"),
        P(None, "chan"),
        P("chan"),
    )
    return jax.shard_map(
        local, mesh=mesh, in_specs=placed, out_specs=P("seq", "chan"), check_vma=False
    )
```

```python
import jax
import jax.numpy as jnp
from jax import lax
from jax.experimental import pallas as pl
from jax.experimental.pallas import tpu as pltpu
from jax.sharding import PartitionSpec as P

MESH = pl.DeviceIdType.MESH
F32, BF16 = jnp.float32, jnp.bfloat16
ROWS = 256
CH = 512
DEPTH = 64
MODES = 16
SEQ = 16384.0
SUBS = 8
STEPS = ROWS // SUBS
TOP = 16
SENDS, RECVS = 44, 81


def rounded(value):
    return value.astype(BF16).astype(F32)


def kernel(
    tok, w, taps, res, poles, skip, out,
    wbuf, xbuf, acc, legs, gbuf, ybuf, qbuf, obuf, ends, prefix, decay, tail_w, head_w, powers,
    state, sib_state, c_msg, y_in, z_msg, z_in, k_msg, k_in, carry, packed, last_out, last_in, last,
    send, recv, loc,
):
    s, c = lax.axis_index("seq"), lax.axis_index("chan")
    k, zh = lax.rem(s, 2), lax.rem(lax.div(s, 2), 2)
    y, x = lax.rem(lax.div(s, 4), 4), lax.div(s, 16)

    def at(px=x, py=y, pzh=zh, pk=k, pc=c):
        return (((px * 4 + py) * 2 + pzh) * 2 + pk, pc)

    def xs(d):
        return lax.rem(x + d + 4, 4)

    def ys(d):
        return lax.rem(y + d + 4, 4)

    over = lax.div(c + 4, 8)
    far_c = lax.rem(c + 4, 8)
    z_up = at(pzh=lax.rem(zh + over, 2), pc=far_c)
    z_dn = at(pzh=lax.rem(zh + over + 1, 2), pc=far_c)
    sibling = at(pk=1 - k)
    opposite = at(pzh=1 - zh)
    up, dn = lax.rem(c + 1, 8), lax.rem(c + 7, 8)
    after, before = (lax.rem(s + 1, 64), c), (lax.rem(s + 63, 64), c)

    barrier = pltpu.get_barrier_semaphore()
    partners = [sibling, opposite, z_up, z_dn, (s, up), (s, dn), after, before]
    steps = [(dx, dy) for dx in range(4) for dy in range(4) if dx or dy]
    partners += [at(px=xs(dx), py=ys(dy)) for dx, dy in steps]
    for partner in partners:
        pl.semaphore_signal(barrier, inc=1, device_id=partner, device_id_type=MESH)
    pl.semaphore_wait(barrier, len(partners))

    sent, done, send_ids, recv_ids = [], [], {}, {}

    def start(src, dst, to, cond=None, out_group=None, in_group=None):
        out_id = send_ids.setdefault(out_group or ("one", len(send_ids)), len(send_ids))
        in_id = recv_ids.setdefault(in_group or ("one", len(recv_ids)), len(recv_ids))
        copy = pltpu.make_async_remote_copy(
            src_ref=src, dst_ref=dst, send_sem=send.at[out_id], recv_sem=recv.at[in_id],
            device_id=to, device_id_type=MESH,
        )
        if cond is None:
            copy.start()
        else:
            pl.when(cond)(lambda: copy.start())
        if out_group is None:
            sent.append((copy, cond))
        return copy

    def of_group(blocks, out_group=None, in_group=None):
        ref = {
            1: wbuf.at[0, 0, 0, 0], 2: wbuf.at[0, 0, 0], 4: wbuf.at[0, 0],
            8: wbuf.at[0, pl.ds(0, 4), 0], 16: wbuf.at[0], 32: wbuf.at[pl.ds(0, 2)],
        }[blocks]
        return pltpu.make_async_remote_copy(
            src_ref=ref, dst_ref=ref, send_sem=send.at[send_ids.get(out_group, 0)],
            recv_sem=recv.at[recv_ids.get(in_group, 0)], device_id=sibling, device_id_type=MESH,
        )

    def drain():
        for copy, cond in sent[len(done) :]:
            if cond is None:
                copy.wait_send()
            else:
                pl.when(cond)(lambda copy=copy: copy.wait_send())
            done.append(copy)

    def drain_groups():
        for copy, cond in chained.values():
            pl.when(cond)(lambda copy=copy: copy.wait_send())
        for group, blocks in (("leg", 2), ("near", 4), ("far", 2), ("turned", 16), ("passed", 8), ("sib", 32)):
            of_group(blocks, out_group=group).wait_send()

    chain, chained = {}, {}

    def pass_along(j, key, ref):
        low, high = lax.rem(c - j + 9, 8), lax.rem(c + j - 1, 8)
        for way, block, to, cond in (
            (0, low, up, (c < 7) & (c >= j - 1)),
            (1, high, dn, (c > 0) & (c + j <= 8)),
        ):
            if (j - 3, key, way) in chain:
                before_cond = (c < 7) & (c >= j - 4) if way == 0 else (c > 0) & (c + j <= 11)
                old = chain[j - 3, key, way]
                pl.when(before_cond)(lambda: old.wait_send())
            chain[j, key, way] = start(ref(block), ref(block), (s, to), cond, ("chain", j % 3, key, way))
            chained[j % 3, key, way] = chain[j, key, way], cond

    def arrive(j, key):
        pl.when(c >= j)(lambda: chain[j, key, 0].wait_recv())
        pl.when(c + j <= 7)(lambda: chain[j, key, 1].wait_recv())

    def tok_send(j, h):
        pass_along(j, h, lambda block: xbuf.at[block, pl.ds(2 * h, 2)])

    def last_send(j):
        pass_along(j, "last", lambda block: last.at[block])

    def tok_step(j, h):
        arrive(j, h)
        if j < 7:
            tok_send(j + 1, h)

    def last_step(j):
        arrive(j, "last")
        if j < 7:
            last_send(j + 1)

    def one(which, d, zz, rows):
        px, py = (xs(d), y) if which == "x" else (x, ys(d))
        return wbuf.at[px, py, zz, k, rows]

    def line(which, d, zz, rows):
        if which == "x":
            return wbuf.at[xs(d), pl.ds(0, 4), zz, k, rows]
        return wbuf.at[pl.ds(0, 4), ys(d), zz, k, rows]

    def to(which, d):
        return at(px=xs(d)) if which == "x" else at(py=ys(d))

    ORDER = (("x", "y", 0), ("y", "x", 32))

    class Gather:
        def __init__(self, zz, name):
            self.zz, self.name = zz, name
            for first, _, r in ORDER:
                rows = pl.ds(r, 32)
                src = w.at[rows] if name == "mine" else one(first, 0, zz, rows)
                for d in (1, -1):
                    self.put(src, one(first, 0, zz, rows), to(first, d), "near")
            for first, second, r in ORDER:
                self.turn(first, second, r, 0, "turned0")

        def put(self, src, dst, where, group, in_group=None):
            start(src, dst, where, out_group=group, in_group=(self.name, in_group or group))

        def got(self, group, blocks):
            of_group(blocks, in_group=(self.name, group)).wait_recv()

        def turn(self, first, second, r, p, group):
            ref = one(first, p, self.zz, pl.ds(r, 32))
            src = w.at[pl.ds(r, 32)] if self.name == "mine" and p == 0 else ref
            for d in (1, -1):
                self.put(src, ref, to(second, d), "turned", group)

        def half(self, r, d):
            return pl.ds(r + (0 if d == 1 else 16), 16)

        def pass_turned(self, p):
            for first, second, r in ORDER:
                for d in (1, -1):
                    px, py = (xs(p), ys(-d)) if second == "y" else (xs(-d), ys(p))
                    ref = wbuf.at[px, py, self.zz, k, self.half(r, d)]
                    self.put(ref, ref, to(second, d), "passed")

        def to_sibling(self, d):
            for _, second, r in ORDER:
                ref = line(second, d, self.zz, pl.ds(r, 32))
                self.put(ref, ref, sibling, "sib")

        def step1(self):
            self.got("near", 2)
            for first, second, r in ORDER:
                for d in (1, -1):
                    ref = one(first, -d, self.zz, self.half(r, d))
                    self.put(ref, ref, to(first, d), "far")
                    self.turn(first, second, r, -d, "turned1")
            self.got("turned0", 2)
            self.pass_turned(0)

        def step2(self):
            self.got("far", 1)
            for first, second, r in ORDER:
                self.turn(first, second, r, 2, "turned2")
            self.to_sibling(0)
            self.got("turned1", 4)
            self.pass_turned(1)
            self.pass_turned(-1)

        def step3(self):
            self.got("turned2", 2)
            self.pass_turned(2)
            self.to_sibling(1)
            self.to_sibling(-1)

        def step4(self):
            self.got("passed", 4)
            self.to_sibling(2)

        def wait_sibling(self):
            self.got("sib", 16)

    def leg(way, r):
        return start(w.at[pl.ds(32 * way + r, 16)], legs.at[way, pl.ds(r, 16)], z_dn if way else z_up, None, "leg")

    def next_leg(way, r):
        zz = lax.rem(zh + over, 2)
        dst = wbuf.at[x, y, zz if way else 1 - zz, k, pl.ds(32 * way + r, 16)]
        return start(legs.at[way, pl.ds(r, 16)], dst, z_dn if way else z_up, None, "leg", "leg2")

    leg1 = [leg(way, r) for r in (0, 16) for way in (0, 1)]
    mine = Gather(zh, "mine")
    keep_w = pltpu.make_async_copy(w, wbuf.at[x, y, zh, k], loc.at[0])
    keep_w.start()
    packed[...] = jnp.zeros_like(packed)
    for j in range(4):
        xbuf[c, j] = tok[:, j * 128 : (j + 1) * 128]
        packed[2 * j : 2 * j + 2, :] = tok[ROWS - 16 :, j * 128 : (j + 1) * 128].astype(F32)[14:, :]
    last_out[...] = packed[...].astype(BF16)
    handed = start(last_out, last_in, after)

    def tables():
        acc[...] = jnp.zeros_like(acc)
        rate = poles[...] * (-1.0 / SEQ)
        decay[...] = jnp.exp(rate)
        powers[0] = jnp.exp(rate * ROWS)
        powers[1] = jnp.exp(rate * (2.0 * ROWS))
        powers[2] = jnp.exp(rate * (4.0 * ROWS))
        sub = lax.broadcasted_iota(jnp.int32, (SUBS, CH), 0).astype(F32)
        for n in range(MODES):
            r = poles[n : n + 1, :] * (-STEPS / SEQ)
            head_w[n] = jnp.exp(r * sub)
            tail_w[n] = jnp.exp(r * (SUBS - 1.0 - sub))

    def add_dot(cc, left, right):
        for g in range(3):
            dot = jnp.dot(left, right(pl.ds(g * CH, CH)), preferred_element_type=F32)
            for lg in range(4):
                acc[4 * g + lg] += dot[:, lg * 128 : (lg + 1) * 128]

    row = lax.broadcasted_iota(jnp.int32, (TOP, 128), 0)

    def features(cc, j):
        top = jnp.where((row >= 2 * j) & (row < 2 * j + 2), last[cc].astype(F32), 0.0).astype(BF16)
        return jnp.concatenate([top, xbuf[cc, j]], axis=0)

    def dot_z(zz, cc):
        px, py = lax.div(cc, 2), lax.rem(cc, 2) * 2
        left = jnp.concatenate([features(cc, zz), features(cc, zz + 2)], axis=1)
        add_dot(cc, left, lambda cols: wbuf[px, pl.ds(py, 2), zz, :, :, cols].reshape(256, CH))

    def dot_y(p, cc):
        px, py = lax.div(cc, 2), lax.rem(cc, 2) * 2 + p
        left = jnp.concatenate([features(cc, 2 * p), features(cc, 2 * p + 1)], axis=1)
        add_dot(cc, left, lambda cols: wbuf[px, py, :, :, :, cols].reshape(256, CH))

    def dots(kind, which, lo, hi):
        def body(j, _):
            pl.when(c >= j)(lambda: kind(which, lax.rem(c - j + 8, 8)))
            pl.when((j > 0) & (c + j <= 7))(lambda: kind(which, lax.rem(c + j, 8)))
            return 0

        lax.fori_loop(lo, hi, body, 0)

    mine.step1()
    for copy, (r, way) in zip(leg1, ((0, 0), (0, 1), (16, 0), (16, 1))):
        copy.wait_recv()
        next_leg(way, r)
    tok_send(1, 0)
    tok_send(1, 1)
    keep_w.wait()
    mine.step2()
    tables()
    mine.step3()
    handed.wait_recv()
    last[c] = jnp.where(s > 0, last_in[...].astype(F32), 0.0).astype(BF16)
    last_send(1)
    tok_step(1, 0)
    of_group(1, in_group="leg2").wait_recv()
    theirs = Gather(1 - zh, "theirs")
    mine.step4()
    tok_step(1, 1)
    last_step(1)
    theirs.step1()
    tok_step(2, 0)
    last_step(2)
    tok_step(2, 1)
    theirs.step2()
    tok_step(3, 0)
    mine.wait_sibling()
    dots(dot_z, zh, 0, 2)
    tok_step(3, 1)
    last_step(3)
    theirs.step3()
    tok_step(4, 0)
    dots(dot_z, zh, 2, 4)
    tok_step(4, 1)
    theirs.step4()
    last_step(4)
    tok_step(5, 0)
    tok_step(5, 1)
    last_step(5)
    dots(dot_z, zh, 4, 6)
    tok_step(6, 0)
    tok_step(6, 1)
    last_step(6)
    theirs.wait_sibling()
    dots(dot_z, 1 - zh, 0, 6)
    dots(dot_z, zh, 6, 7)
    dots(dot_z, 1 - zh, 6, 7)
    tok_step(7, 0)
    last_step(7)
    dots(dot_y, 0, 7, 8)
    tok_step(7, 1)
    dots(dot_y, 1, 7, 8)
    for i in range(12):
        for r in range(2):
            two = [acc[i, 2 * j + r : 2 * j + r + 1, :] for j in range(4)]
            acc[i, TOP - 2 + r : TOP - 1 + r, :] = total(two)

    def lanes(lg):
        return pl.ds(pl.multiple_of(lg * 128, 128), 128)

    def rows_of(ref, lg):
        return [jnp.broadcast_to(ref[n : n + 1, lanes(lg)], (SUBS, 128)) for n in range(MODES)]

    def filter_of(g, lg):
        t = [jnp.broadcast_to(taps[i, g : g + 1, lanes(lg)], (SUBS, 128)) for i in range(3)]

        def load(first):
            return rounded(acc[4 * g + lg, pl.ds(first, SUBS, stride=STEPS), :])

        return lambda p0, p1, p2: t[0] * p0 + t[1] * p1 + t[2] * p2, load

    def gate(fk, fv, k3, v3):
        return rounded(fk(*k3) * fv(*v3))

    def pass_a(lg):
        (fk, lk), (fv, lv) = filter_of(1, lg), filter_of(2, lg)
        a = rows_of(decay, lg)

        def body(i, held):
            k1, k2, v1, v2, st = held
            k0, v0 = lk(TOP + i), lv(TOP + i)
            g = gate(fk, fv, (k0, k1, k2), (v0, v1, v2))
            gbuf[i, :, lanes(lg)] = g
            return k0, k1, v0, v1, tuple(a[n] * st[n] + g for n in range(MODES))

        zero = tuple(jnp.zeros((SUBS, 128), F32) for _ in range(MODES))
        held = lax.fori_loop(0, STEPS, body, (lk(TOP - 1), lk(TOP - 2), lv(TOP - 1), lv(TOP - 2), zero), unroll=8)
        for n in range(MODES):
            ends[n, :, lanes(lg)] = held[4][n]
            state[n : n + 1, lanes(lg)] = jnp.sum(tail_w[n, :, lanes(lg)] * held[4][n], axis=0, keepdims=True)

    half = pl.ds(pl.multiple_of(k * 256, 256), 256)
    other = pl.ds(pl.multiple_of((1 - k) * 256, 256), 256)
    own_groups, other_groups = (2 * k, 2 * k + 1), (2 - 2 * k, 3 - 2 * k)
    for lg in other_groups:
        pass_a(lg)
    first = start(state.at[:, other], sib_state.at[:, other], sibling)
    for lg in own_groups:
        pass_a(lg)
    second = start(state.at[:, half], sib_state.at[:, half], sibling)

    def pass_b(lg):
        fq, lq = filter_of(0, lg)
        a, r = rows_of(decay, lg), rows_of(res, lg)
        gain = jnp.broadcast_to(skip[0:1, lanes(lg)], (SUBS, 128))

        def body(i, held):
            q1, q2, st = held
            q0 = lq(TOP + i)
            qbuf[i, :, lanes(lg)] = fq(q0, q1, q2)
            g = gbuf[i, :, lanes(lg)]
            st = tuple(a[n] * st[n] + g for n in range(MODES))
            ybuf[i, :, lanes(lg)] = total([r[n] * st[n] for n in range(MODES)] + [gain * g])
            return q0, q1, st

        zero = tuple(jnp.zeros((SUBS, 128), F32) for _ in range(MODES))
        lax.fori_loop(0, STEPS, body, (lq(TOP - 1), lq(TOP - 2), zero), unroll=2)
        sub = lax.broadcasted_iota(jnp.int32, (SUBS, 128), 0)

        def down(value, by):
            return jnp.where(sub >= by, pltpu.roll(value, by, 0), 0.0)

        for n in range(MODES):
            v = down(ends[n, :, lanes(lg)], 1)
            for by in (1, 2, 4):
                v = v + head_w[n, by : by + 1, lanes(lg)] * down(v, by)
            prefix[n, :, lanes(lg)] = v

    first.wait_recv()
    own, sib = state[:, half], sib_state[:, half]
    chip = powers[0, :, half] * jnp.where(k == 0, own, sib) + jnp.where(k == 0, sib, own)
    c_msg[...] = chip
    q = 4 * x + y
    level = []
    for dx, dy in steps:
        later = 4 * xs(dx) + ys(dy) > q
        level.append(start(c_msg, y_in.at[q], at(px=xs(dx), py=ys(dy)), later))
    pass_b(0)
    pass_b(1)
    drain()
    drain_groups()
    for (dx, dy), copy in zip(steps, level):
        pl.when(4 * xs(-dx) + ys(-dy) < q)(lambda copy=copy: copy.wait_recv())
    d4 = powers[2, :, half]
    plane = lax.fori_loop(0, q, lambda i, got: got * d4 + y_in[i], jnp.zeros_like(chip))
    z_msg[...] = jnp.where(zh == 0, d4 * plane + chip, plane)
    level = start(z_msg, z_in, opposite)
    second.wait_recv()
    pass_b(2)
    pass_b(3)
    level.wait_recv()
    into = powers[1, :, half] * plane + z_in[...]
    k_msg[...] = into
    level = start(k_msg, k_in, sibling)

    def keep(where, value):
        carry[:, where] = jnp.where(k == 0, value, powers[0, :, where] * value + sib_state[:, where])

    keep(half, into)

    def pass_c(lg):
        a, r = rows_of(decay, lg), rows_of(res, lg)
        ws = tuple(
            r[n] * (prefix[n, :, lanes(lg)] + head_w[n, :, lanes(lg)] * carry[n : n + 1, lanes(lg)])
            for n in range(MODES)
        )

        def body(i, ws):
            ws = tuple(a[n] * ws[n] for n in range(MODES))
            value = ybuf[i, :, lanes(lg)] + total(list(ws))
            obuf[lg, pl.ds(i, SUBS, stride=STEPS), :] = qbuf[i, :, lanes(lg)] * value
            return ws

        lax.fori_loop(0, STEPS, body, ws, unroll=8)
        out[:, lanes(lg)] = obuf[lg].astype(BF16)

    for lg in own_groups:
        pass_c(lg)
    level.wait_recv()
    keep(other, k_in[...])
    for lg in other_groups:
        pass_c(lg)

    drain()


def total(values):
    while len(values) > 1:
        values = [a + b for a, b in zip(values[::2], values[1::2])] + values[len(values) & ~1 :]
    return values[0]


def local(tokens, w_in, short_taps, residues, poles, skip_gain):
    vmem = pl.BlockSpec(memory_space=pltpu.VMEM)
    block = pltpu.VMEM((STEPS, SUBS, CH), F32)
    table = pltpu.VMEM((MODES, SUBS, CH), F32)
    full, part = pltpu.VMEM((MODES, CH), F32), pltpu.VMEM((MODES, CH // 2), F32)
    last = pltpu.VMEM((16, 128), BF16)
    return pl.pallas_call(
        kernel,
        out_shape=jax.ShapeDtypeStruct((ROWS, CH), BF16),
        in_specs=[vmem] * 6,
        out_specs=vmem,
        scratch_shapes=[
            pltpu.VMEM((4, 4, 2, 2, DEPTH, 3 * CH), BF16),
            pltpu.VMEM((8, 4, ROWS, 128), BF16),
            pltpu.VMEM((12, TOP + ROWS, 128), F32),
            pltpu.VMEM((2, DEPTH // 2, 3 * CH), BF16),
            block, block, block,
            pltpu.VMEM((4, ROWS, 128), F32),
            table, table, full, table, table,
            pltpu.VMEM((3, MODES, CH), F32),
            full, full, part, pltpu.VMEM((16, MODES, CH // 2), F32), part, part, part, part, full,
            pltpu.VMEM((16, 128), F32), last, last, pltpu.VMEM((8, 16, 128), BF16),
            pltpu.SemaphoreType.DMA((SENDS,)),
            pltpu.SemaphoreType.DMA((RECVS,)),
            pltpu.SemaphoreType.DMA((1,)),
        ],
        compiler_params=pltpu.CompilerParams(
            collective_id=0, has_side_effects=True, vmem_limit_bytes=40 * 1024 * 1024
        ),
    )(tokens, w_in.reshape(DEPTH, 3 * CH), short_taps, residues, poles, skip_gain.reshape(1, CH))


def solution(mesh):
    placed = (
        P("seq", "chan"),
        P("seq", None, "chan"),
        P(None, None, "chan"),
        P(None, "chan"),
        P(None, "chan"),
        P("chan"),
    )
    return jax.shard_map(
        local, mesh=mesh, in_specs=placed, out_specs=P("seq", "chan"), check_vma=False
    )
```
